32 devices in a mesh: gx: 4 (over y, core), gy: 8 (over z, x).
Axes of the slice: x: 2, y: 2, z: 4, core: 2. Of those that a mesh axis runs over, the one named last changes fastest.
Arguments:
- velocity: float32 [3, 32, 64, 512], P(None, 'gx', 'gy'), may hold values from -6 to 6
- stress: float32 [6, 32, 64, 512], P(None, 'gx', 'gy'), may hold values from -6 to 6
- lame_lambda: float32 [32, 64, 512], P('gx', 'gy'), may hold values from 0.5 to 5
- lame_mu: float32 [32, 64, 512], P('gx', 'gy'), may hold values from 0.5 to 5
- node_mass: float32 [32, 64, 512], P('gx', 'gy'), may hold values from 0.5 to 2
- displacement: float32 [3, 32, 64, 512], P(None, 'gx', 'gy'), may hold values from -0.75 to 0.75
- seg_elem: int32 [65536], P(('gx', 'gy')), may hold values from 0 to 32767
- seg_bucket: int32 [65536, 1], P(('gx', 'gy')), may hold values from 0 to 31; in each aligned block of 2048 rows (0 to 2047, 2048 to 4095, ...) at most 128 rows name the same one
- slave_points: float32 [3, 16384], P(None, ('gx', 'gy')), may hold values from 0.8 to 1.2
- candidates: int32 [4, 16384], P(None, ('gx', 'gy')), may hold values from 0 to 4095
Outputs:
- new_stress: float32 [6, 32, 64, 512], P(None, 'gx', 'gy')
- acceleration: float32 [3, 32, 64, 512], P(None, 'gx', 'gy')
- slave_force: float32 [3, 16384], P(None, ('gx', 'gy'))
The draws below stay inside these ranges and needn't reach their ends.
Inputs may be any that keep to these rules, and one draw needn't show every extreme that they name: `seg_bucket`: in the rows of one device no bucket is named more than 128 times. `candidates`: A slot index into the 32 x 128 segment slots of the slave's own bucket, source device major; a slot holding no segment contributes nothing.
All inputs are finite; a program needn't handle non-finite values.
Results may differ from the reference program's by a relative error of at most 0.0003.
Values sent between devices are 32-bit elements; how exact they have to be, the bound alone decides.
A program may use at most 128 MiB of HBM per device.

```python
import math
import jax
import jax.numpy as jnp
import numpy as np
from jax import lax

CX = 8
CY = 8
CZ = 512
SEG_DEV = 2048
SLAVE_DEV = 512
K = 4
NX = 32
NY = 64
SEGS = 65536
SLAVES = 16384
CAP = 128
N_GX = 4
N_GY = 8
DEVICES = 32


def with_ends(entries, key, least, top_value):
    longest = entries.shape.index(max(entries.shape))
    spots = []
    for shift in (0, 1):
        where = [jax.random.randint(jax.random.fold_in(key, axis), (), 0, length) for axis, length in enumerate(entries.shape)]
        where[longest] = (where[longest] + shift) % entries.shape[longest]
        spots.append(tuple(where))
    return entries.at[spots[0]].set(least).at[spots[1]].set(top_value)


def level_of(key, extent, cuts, smallest, top_value):
    loudness = 1.0
    for dim, blocks in cuts:
        draws = jax.random.uniform(jax.random.fold_in(jax.random.fold_in(key, 6), dim), (blocks,), jnp.float32, smallest / len(cuts), top_value / len(cuts))
        loudness = loudness * jnp.repeat(jnp.exp(draws), extent[dim] // blocks).reshape((-1,) + (1,) * (len(extent) - 1 - dim))
    return loudness


def shared_out(stream_key, own, number, rows, count, top, limit, lean):
    sequence = jax.random.permutation(stream_key, count)
    heavy_load, common = shares(count, rows * top, limit, lean, True), shares(count, rows * top, limit, lean, False)
    places = jnp.arange(count)

    def named(sizes, rotation):
        used = int((sizes > 0).sum())
        fixed = max(1, used // 4)
        passed = fixed + (places - fixed + rotation * (used - fixed)) % max(1, count - fixed)
        return jnp.zeros((count,), jnp.int32).at[sequence[jnp.where(places < fixed, places, passed)]].set(jnp.asarray(sizes, jnp.int32))

    sizes = jnp.where(number % 4 == 0, named(heavy_load, number // 4), named(common, number - number // 4 - 1))
    mixed = jax.random.permutation(jax.random.fold_in(own, 3), count)
    donor, receiver = mixed[0:count // 2 * 2:2], mixed[1:count // 2 * 2:2]
    slack = jnp.minimum(sizes[donor] - 1, limit - sizes[receiver]) // 2
    slack = jnp.where((donor == sequence[0]) | (receiver == sequence[0]) | (sizes[receiver] == 0), 0, jnp.maximum(slack, 0))
    passed = jax.random.randint(jax.random.fold_in(own, 4), (count // 2,), 0, 1 << 20) % (slack + 1)
    sizes = sizes.at[donor].add(-passed).at[receiver].add(passed)
    members = jnp.searchsorted(jnp.cumsum(sizes), jnp.arange(rows * top), side="right").astype(jnp.int32)
    listing = members.reshape(top, rows).T
    listing = listing[jax.random.permutation(jax.random.fold_in(own, 1), rows)]
    rotation = jax.random.randint(jax.random.fold_in(own, 2), (rows, 1), 0, top)
    return jnp.take_along_axis(listing, (jnp.arange(top)[None, :] + rotation) % top, axis=1)


def shares(count, total, bound, slope, full):
    weights = [(1 << 20) // math.isqrt(rank ** slope) + 1 for rank in range(1, count + 1)]
    largest = bound if full else min(bound, max(-(-total // count), total * weights[0] // sum(weights)))
    least = 1 if total - largest >= count - 1 else 0
    counts, rest = [largest] + [least] * (count - 1), total - largest - least * (count - 1)
    while rest > 0:
        free = [i for i in range(1, count) if counts[i] < largest] or [i for i in range(1, count) if counts[i] < bound]
        mass, remaining = sum([weights[i] for i in free]), rest
        for i in free:
            extra = min(bound - counts[i], max(1, remaining * weights[i] // mass), rest)
            counts[i] = counts[i] + extra
            rest = rest - extra
    return np.array(counts)


def centred(rng, dims, spread, reach, shards=(), kind=jnp.bfloat16):
    level = level_of(rng, dims, shards, -0.22, 0.18) if shards else 1.0
    entries = jax.random.normal(rng, dims, jnp.float32) * spread * level
    return jnp.minimum(jnp.maximum(entries, -reach), reach).astype(kind)


def setup_inputs(seed: int = 0) -> dict:
    key_of = jax.random.split(jax.random.key(seed), 11)
    velocity = centred(key_of[0], (3, NX, NY, CZ), 1.0, 6.0, ((1, 4), (2, 8)), jnp.float32)
    stress = centred(key_of[1], (6, NX, NY, CZ), 1.0, 6.0, ((1, 4), (2, 8)), jnp.float32)
    lame_lambda = jnp.clip(jnp.exp(math.log(5.0) - 2.3025851 * jax.random.uniform(key_of[2], (NX, NY, CZ), jnp.float32) ** level_of(key_of[2], (NX, NY, CZ), ((0, 4), (1, 8)), -0.2, 0.2)), 0.5, 5.0)
    lame_mu = jnp.clip(jnp.exp(math.log(5.0) - 2.3025851 * jax.random.uniform(key_of[3], (NX, NY, CZ), jnp.float32) ** level_of(key_of[3], (NX, NY, CZ), ((0, 4), (1, 8)), -0.2, 0.2)), 0.5, 5.0)
    node_mass = jnp.clip(jnp.exp(math.log(2.0) - 1.3862944 * jax.random.uniform(key_of[4], (NX, NY, CZ), jnp.float32) ** level_of(key_of[4], (NX, NY, CZ), ((0, 4), (1, 8)), -0.2, 0.2)), 0.5, 2.0)
    displacement = centred(key_of[5], (3, NX, NY, CZ), 0.05, 0.75, ((1, 4), (2, 8)), jnp.float32)
    seg_elem = with_ends(jax.random.randint(key_of[6], (SEGS,), 0, CX * CY * CZ), jax.random.fold_in(key_of[6], 1), 0, (CX * CY * CZ) - 1).astype(jnp.int32)
    seg_bucket_keys = jax.random.split(jax.random.fold_in(key_of[7], 1), SEGS // SEG_DEV)
    seg_bucket_turns = jax.random.permutation(jax.random.fold_in(key_of[7], 3), SEGS // SEG_DEV)
    seg_bucket = jax.vmap(lambda own, number: shared_out(jax.random.fold_in(key_of[7], 2), own, number, SEG_DEV, DEVICES, 1, CAP, 2))(seg_bucket_keys, seg_bucket_turns).reshape((SEGS, 1))
    slave_points = jnp.clip(0.8 + 0.40000004 * jax.random.uniform(key_of[8], (3, SLAVES), jnp.float32) ** level_of(key_of[8], (3, SLAVES), ((1, 32),), -0.2, 0.2), 0.8, 1.2)
    candidates = with_ends(jax.random.randint(key_of[9], (K, SLAVES), 0, DEVICES * CAP), jax.random.fold_in(key_of[9], 1), 0, (DEVICES * CAP) - 1).astype(jnp.int32)
    return {"velocity": velocity, "stress": stress, "lame_lambda": lame_lambda, "lame_mu": lame_mu, "node_mass": node_mass, "displacement": displacement, "seg_elem": seg_elem, "seg_bucket": seg_bucket, "slave_points": slave_points, "candidates": candidates}


time_step = 0.1
penalty = 10.0


def element_pass(extended, stress, lame_lambda, lame_mu):
    size_x = extended.shape[1] - 1
    size_y = extended.shape[2] - 1
    size_z = extended.shape[3] - 1
    nodal = extended[0:3]

    def corner_vel(side_x, side_y, side_z):
        return nodal[:, side_x:side_x + size_x, side_y:side_y + size_y, side_z:side_z + size_z]

    grad_x = 0.25 * sum(corner_vel(1, p, q) - corner_vel(0, p, q) for p in (0, 1) for q in (0, 1))
    grad_y = 0.25 * sum(corner_vel(p, 1, q) - corner_vel(p, 0, q) for p in (0, 1) for q in (0, 1))
    grad_z = 0.25 * sum(corner_vel(p, q, 1) - corner_vel(p, q, 0) for p in (0, 1) for q in (0, 1))
    rate_xx = grad_x[0]
    rate_yy = grad_y[1]
    rate_zz = grad_z[2]
    rate_yz = 0.5 * (grad_z[1] + grad_y[2])
    rate_xz = 0.5 * (grad_z[0] + grad_x[2])
    rate_xy = 0.5 * (grad_y[0] + grad_x[1])
    volume_rate = rate_xx + rate_yy + rate_zz
    stress_xx = stress[0] + time_step * (lame_lambda * volume_rate + 2.0 * lame_mu * rate_xx)
    stress_yy = stress[1] + time_step * (lame_lambda * volume_rate + 2.0 * lame_mu * rate_yy)
    stress_zz = stress[2] + time_step * (lame_lambda * volume_rate + 2.0 * lame_mu * rate_zz)
    stress_yz = stress[3] + time_step * 2.0 * lame_mu * rate_yz
    stress_xz = stress[4] + time_step * 2.0 * lame_mu * rate_xz
    stress_xy = stress[5] + time_step * 2.0 * lame_mu * rate_xy
    new_stress = jnp.stack([stress_xx, stress_yy, stress_zz, stress_yz, stress_xz, stress_xy])
    tensor = ((stress_xx, stress_xy, stress_xz), (stress_xy, stress_yy, stress_yz), (stress_xz, stress_yz, stress_zz))
    forces = jnp.zeros((3, size_x + 1, size_y + 1, size_z + 1), extended.dtype)
    for side_x in (0, 1):
        for side_y in (0, 1):
            for side_z in (0, 1):
                sign_x = 2.0 * side_x - 1.0
                sign_y = 2.0 * side_y - 1.0
                sign_z = 2.0 * side_z - 1.0
                part = jnp.stack([-0.25 * (sign_x * tensor[row][0] + sign_y * tensor[row][1] + sign_z * tensor[row][2]) for row in range(3)])
                forces = forces + jnp.pad(part, ((0, 0), (side_x, 1 - side_x), (side_y, 1 - side_y), (side_z, 1 - side_z)))
    return new_stress, forces


def seg_geometry(corners):
    low_low = corners[0:3]
    high_low = corners[3:6]
    high_high = corners[6:9]
    low_high = corners[9:12]
    centre = 0.25 * (low_low + high_low + high_high + low_high)
    first = high_high - low_low
    second = low_high - high_low
    area = 0.5 * jnp.stack([first[1] * second[2] - first[2] * second[1],
                            first[2] * second[0] - first[0] * second[2],
                            first[0] * second[1] - first[1] * second[0]])
    return centre, area


def slot_rank(bucket, devices):
    onehot = (bucket[:, None] == jnp.arange(devices, dtype=jnp.int32)[None, :]).astype(jnp.int32)
    running = jnp.cumsum(onehot, axis=0)
    return (jnp.sum(running * onehot, axis=1) - 1).astype(jnp.int32)


def reference(velocity, stress, lame_lambda, lame_mu, node_mass, displacement, seg_elem, seg_bucket, slave_points, candidates):
    devices = N_GX * N_GY
    extended = jnp.pad(jnp.concatenate([velocity, displacement], 0), ((0, 0), (0, 1), (0, 1), (0, 1)))
    new_stress, forces = element_pass(extended, stress, lame_lambda, lame_mu)
    bucket = seg_bucket[:, 0]
    ranks = lax.map(lambda block: slot_rank(block, devices), bucket.reshape(devices, SEG_DEV)).reshape(-1)
    source = jnp.arange(SEGS, dtype=jnp.int32) // SEG_DEV
    cell_i = seg_elem // (CY * CZ) + (source // N_GY) * CX
    cell_j = (seg_elem // CZ) % CY + (source % N_GY) * CY
    cell_k = seg_elem % CZ
    flat_disp = extended[3:6].reshape(3, -1)
    offsets = ((0, 0), (1, 0), (1, 1), (0, 1))
    indices = []
    pieces = []
    for off_a, off_b in offsets:
        index = (((cell_i + off_a) * (NY + 1) + cell_j + off_b) * (CZ + 1) + cell_k + 1).astype(jnp.int32)
        indices.append(index)
        shift_vec = jnp.array([off_a, off_b, 1.0], jnp.float32)[:, None]
        pieces.append(flat_disp[:, index] + shift_vec)
    centre, area = seg_geometry(jnp.concatenate(pieces, 0))
    per_bucket = devices * CAP
    slot = (bucket * per_bucket + source * CAP + ranks).astype(jnp.int32)
    total = devices * per_bucket
    table_centre = jnp.zeros((3, total), jnp.float32).at[:, slot].set(centre)
    table_area = jnp.zeros((3, total), jnp.float32).at[:, slot].set(area)
    owner = jnp.arange(SLAVES, dtype=jnp.int32) // SLAVE_DEV
    global_slot = (owner[None, :] * per_bucket + candidates).astype(jnp.int32)
    near_centre = table_centre[:, global_slot]
    near_area = table_area[:, global_slot]
    gap = jnp.sum(near_area * (slave_points[:, None, :] - near_centre), axis=0)
    push = penalty * jnp.maximum(-gap, 0.0)[None] * near_area
    slave_force = jnp.sum(push, axis=1)
    reaction = jax.ops.segment_sum(-push.reshape(3, -1).T, global_slot.reshape(-1), num_segments=total).T
    quarter = 0.25 * reaction[:, slot]
    flat_forces = forces.reshape(3, -1)
    for index in indices:
        flat_forces = flat_forces.at[:, index].add(quarter)
    forces = flat_forces.reshape(forces.shape)[:, :NX, :NY, :CZ]
    acceleration = forces / node_mass[None]
    return new_stress, acceleration, slave_force
```

```python
import functools

import jax
import jax.numpy as jnp
from jax import lax
from jax.experimental import pallas as pl
from jax.experimental.pallas import tpu as pltpu
from jax.sharding import PartitionSpec as P

time_step = 0.1
penalty = 10.0
LANES = 128
F32 = jnp.float32
BF16 = jnp.bfloat16
VMEM = pl.BlockSpec(memory_space=pltpu.VMEM)
NN = (((1,), (0,)), ((), ()))
NT = (((1,), (1,)), ((), ()))


def split_index(value, size):
    if size & (size - 1) == 0:
        return value >> (size.bit_length() - 1), value & (size - 1)
    return value // size, value % size


def two_terms(value):
    high = value.astype(BF16)
    return high, (value - high.astype(F32)).astype(BF16)


def dot(left, right, dims):
    return lax.dot_general(left, right, dims, preferred_element_type=F32)


def one_hot(row, count):
    return lax.broadcasted_iota(jnp.int32, (count, row.shape[1]), 0) == row


def next_row(tile, last):
    rows = tile.shape[0]
    rolled = pltpu.roll(tile, rows - 1, 0)
    return jnp.where(lax.broadcasted_iota(jnp.int32, tile.shape, 0) == rows - 1, last, rolled)


def previous_row(tile):
    rolled = pltpu.roll(tile, 1, 0)
    return jnp.where(lax.broadcasted_iota(jnp.int32, tile.shape, 0) == 0, 0.0, rolled)


def next_lane(tile):
    lanes = tile.shape[1]
    rolled = pltpu.roll(tile, lanes - 1, 1)
    return jnp.where(lax.broadcasted_iota(jnp.int32, tile.shape, 1) == lanes - 1, 0.0, rolled)


def previous_lane(tile):
    rolled = pltpu.roll(tile, 1, 1)
    return jnp.where(lax.broadcasted_iota(jnp.int32, tile.shape, 1) == 0, 0.0, rolled)


def index_kernel(devices, capacity, size_z, elem, bucket, out):
    count = elem.shape[1]
    row, depth = split_index(elem[...], size_z)
    out[0:1] = depth + 1
    out[1:2] = row
    tri = (
        lax.broadcasted_iota(jnp.int32, (LANES, LANES), 0)
        <= lax.broadcasted_iota(jnp.int32, (LANES, LANES), 1)
    ).astype(F32).astype(BF16)
    carry = jnp.zeros((devices, 1), F32)
    for start in range(0, count, LANES):
        here = bucket[:, start : start + LANES]
        hot = one_hot(here, devices).astype(F32)
        running = dot(hot.astype(BF16), tri, NN)
        rank = jnp.sum(hot * (running + carry), axis=0, keepdims=True) - 1.0
        carry = carry + running[:, LANES - 1 : LANES]
        target = here * capacity + rank.astype(jnp.int32)
        high, low = split_index(target, LANES)
        out[2:3, start : start + LANES] = high
        out[3:4, start : start + LANES] = low
    out[4:8] = jnp.zeros((4, count), jnp.int32)


def spread(values, high, groups):
    rows, lanes = values.shape
    which = lax.broadcasted_iota(jnp.int32, (groups, rows, lanes), 0)
    kept = jnp.where(which == high[None], values[None], 0.0)
    return kept.reshape(groups * rows, lanes)


def picked(table, high, groups):
    rows = table.shape[0] // groups
    lanes = table.shape[1]
    total = jnp.zeros((rows, lanes), F32)
    for group in range(groups):
        total = jnp.where(high == group, table[group * rows : (group + 1) * rows], total)
    return total


def geometry_kernel(chunk, own, ghost_x, ghost_y, ghost_c, index, out, faces, payload):
    size_x, size_y, size_z = own.shape[1:]
    groups = out.shape[0]
    count = index.shape[1]

    def plane(comp, i):
        return own[comp, i] if i < size_x else ghost_x[comp]

    def last_row(comp, i):
        return ghost_y[comp, i : i + 1] if i < size_x else ghost_c[comp : comp + 1]

    for i in range(size_x):
        p, q = [], []
        for comp in range(3):
            low, high = plane(comp, i), plane(comp, i + 1)
            low_next = next_row(low, last_row(comp, i))
            high_next = next_row(high, last_row(comp, i + 1))
            faces[comp, i] = 0.25 * ((low + high) + (low_next + high_next))
            p.append(high_next - low)
            q.append(low_next - high)
        faces[3, i] = 0.5 * ((1.0 + p[1]) * q[2] - p[2] * (1.0 + q[1]))
        faces[4, i] = 0.5 * (p[2] * (q[0] - 1.0) - (1.0 + p[0]) * q[2])
        faces[5, i] = 0.5 * (p[0] + p[1] + q[1] - q[0] + p[0] * q[1] - p[1] * q[0])
    rows = size_x * size_y
    high, low = two_terms(faces[...].reshape(6 * rows, size_z))
    total = jnp.zeros((groups * 8, LANES), F32)
    payload[6:7] = jnp.ones((1, chunk), F32)
    payload[7:8] = jnp.zeros((1, chunk), F32)
    for start in range(0, count, chunk):
        here = slice(start, start + chunk)
        hot = one_hot(index[0:1, here], size_z).astype(F32).astype(BF16)
        near = dot(high, hot, NN) + dot(low, hot, NN)
        hot_row = one_hot(index[1:2, here], rows)
        for comp in range(6):
            payload[comp : comp + 1] = jnp.sum(
                jnp.where(hot_row, near[comp * rows : (comp + 1) * rows], 0.0), axis=0, keepdims=True
            )
        slot = index[2:3, here]
        hot_low = one_hot(index[3:4, here], LANES).astype(F32).astype(BF16)
        values = payload[...]
        part = values.astype(BF16).astype(F32)
        total += dot(spread(part, slot, groups).astype(BF16), hot_low, NT)
        total += dot(spread(values - part, slot, groups).astype(BF16), hot_low, NT)
    out[...] = total.reshape(out.shape)


def stress_kernel(
    own, ghost_x, ghost_y, ghost_c, stress, lame_lambda, lame_mu,
    new_stress, force, force_x, force_y, force_c,
):
    size_x = own.shape[1]
    size_y = own.shape[2]

    def plane(comp, i):
        tile = own[comp, i] if i < size_x else ghost_x[comp]
        last = ghost_y[comp, i : i + 1] if i < size_x else ghost_c[comp : comp + 1]
        after = next_row(tile, last)
        both, change = tile + after, after - tile
        return both + next_lane(both), change + next_lane(change), next_lane(both) - both

    low = [plane(comp, 0) for comp in range(3)]
    carry = None
    for i in range(size_x):
        high = [plane(comp, i + 1) for comp in range(3)]
        grad_x = [high[c][0] - low[c][0] for c in range(3)]
        grad_y = [high[c][1] + low[c][1] for c in range(3)]
        grad_z = [high[c][2] + low[c][2] for c in range(3)]
        low = high
        shear = (0.5 * time_step) * lame_mu[i]
        volume = (0.25 * time_step) * lame_lambda[i] * (grad_x[0] + grad_y[1] + grad_z[2])
        s_xx = stress[0, i] + (volume + shear * grad_x[0])
        s_yy = stress[1, i] + (volume + shear * grad_y[1])
        s_zz = stress[2, i] + (volume + shear * grad_z[2])
        half = 0.5 * shear
        s_yz = stress[3, i] + half * (grad_z[1] + grad_y[2])
        s_xz = stress[4, i] + half * (grad_z[0] + grad_x[2])
        s_xy = stress[5, i] + half * (grad_y[0] + grad_x[1])
        for number, value in enumerate((s_xx, s_yy, s_zz, s_yz, s_xz, s_xy)):
            new_stress[number, i] = value
        tensor = ((s_xx, s_xy, s_xz), (s_xy, s_yy, s_yz), (s_xz, s_yz, s_zz))
        later = []
        for comp in range(3):
            first, second, third = (-0.25 * t for t in tensor[comp])
            first = first + previous_lane(first)
            second = second + previous_lane(second)
            third = previous_lane(third) - third
            near_plus, near_minus = third - second + first, third - second - first
            far_plus, far_minus = third + second + first, third + second - first
            plus = near_plus + previous_row(far_plus)
            minus = near_minus + previous_row(far_minus)
            plus_end = far_plus[size_y - 1 : size_y]
            minus_end = far_minus[size_y - 1 : size_y]
            if carry is not None:
                minus = minus + carry[comp][0]
                minus_end = minus_end + carry[comp][1]
            force[comp, i] = minus
            force_y[comp, i : i + 1] = minus_end
            later.append((plus, plus_end))
        carry = later
    for comp in range(3):
        force_x[comp] = carry[comp][0]
        force_c[comp : comp + 1] = carry[comp][1]


def contact_kernel(arrived, points, candidates, slave_force, reaction):
    groups = arrived.shape[0]
    lanes = points.shape[1]
    high, low = two_terms(arrived[...].reshape(groups * 8, LANES))
    total = jnp.zeros((groups * 8, LANES), F32)
    pushed = [jnp.zeros((1, lanes), F32) for _ in range(3)]
    eight = lax.broadcasted_iota(jnp.int32, (8, lanes), 0)
    for k in range(candidates.shape[0]):
        slot, place = split_index(candidates[k : k + 1], LANES)
        hot = one_hot(place, LANES).astype(F32).astype(BF16)
        near = picked(dot(high, hot, NN) + dot(low, hot, NN), slot, groups)
        rows = [near[r : r + 1] for r in range(7)]
        filled = rows[6]
        offset = (0.5, 0.5, 1.0)
        area = (rows[3], rows[4], rows[5] + filled)
        gap = jnp.zeros((1, lanes), F32)
        for comp in range(3):
            gap = gap + area[comp] * (points[comp : comp + 1] - (rows[comp] + offset[comp] * filled))
        scale = penalty * jnp.maximum(-gap, 0.0)
        values = jnp.zeros((8, lanes), F32)
        for comp in range(3):
            push = scale * area[comp]
            pushed[comp] = pushed[comp] + push
            values = jnp.where(eight == comp, -push, values)
        part = values.astype(BF16).astype(F32)
        total += dot(spread(part, slot, groups).astype(BF16), hot, NT)
        total += dot(spread(values - part, slot, groups).astype(BF16), hot, NT)
    for comp in range(3):
        slave_force[comp : comp + 1] = pushed[comp]
    reaction[...] = total.reshape(reaction.shape)


def nodes_kernel(
    chunk, returned, index, in_force, in_x, in_y, in_c, force, force_x, force_y, force_c
):
    size_x, size_y, size_z = in_force.shape[1:]
    groups = returned.shape[0]
    count = index.shape[1]
    rows = size_x * size_y
    high, low = two_terms(returned[...].reshape(groups * 8, LANES))
    total = jnp.zeros((3 * rows, size_z), F32)
    for start in range(0, count, chunk):
        here = slice(start, start + chunk)
        hot_low = one_hot(index[3:4, here], LANES).astype(F32).astype(BF16)
        near = picked(dot(high, hot_low, NN) + dot(low, hot_low, NN), index[2:3, here], groups)
        quarter = 0.25 * near
        part = quarter.astype(BF16).astype(F32)
        rest = quarter - part
        hot_row = one_hot(index[1:2, here], rows)
        hot = one_hot(index[0:1, here], size_z).astype(F32).astype(BF16)
        for values in (part, rest):
            left = jnp.concatenate(
                [jnp.where(hot_row, values[c : c + 1], 0.0) for c in range(3)], 0
            ).astype(BF16)
            total += dot(left, hot, NT)
    for comp in range(3):
        before = None
        for i in range(size_x):
            at = (comp * size_x + i) * size_y
            tile = total[at : at + size_y]
            both = tile + previous_row(tile)
            end = tile[size_y - 1 : size_y]
            value, value_end = both, end
            if before is not None:
                value, value_end = both + before[0], end + before[1]
            force[comp, i] = in_force[comp, i] + value
            force_y[comp, i : i + 1] = in_y[comp, i : i + 1] + value_end
            before = (both, end)
        force_x[comp] = in_x[comp] + before[0]
        force_c[comp : comp + 1] = in_c[comp : comp + 1] + before[1]


def final_kernel(force, from_x, from_y, from_c, mass, out):
    size_x = force.shape[1]
    first = lax.broadcasted_iota(jnp.int32, force.shape[2:], 0) == 0
    for i in range(size_x):
        inverse = 1.0 / mass[i]
        for comp in range(3):
            end = from_y[comp, i : i + 1]
            value = force[comp, i]
            if i == 0:
                end = end + from_c[comp : comp + 1]
                value = value + from_x[comp]
            out[comp, i] = (value + jnp.where(first, end, 0.0)) * inverse


def call(kernel, outs, *args, scratch=(), flops=0):
    moved = sum(a.size * 4 for a in args) + sum(4 * functools.reduce(lambda x, y: x * y, s) for s, _ in outs)
    return pl.pallas_call(
        kernel,
        out_shape=[jax.ShapeDtypeStruct(s, d) for s, d in outs],
        in_specs=[VMEM] * len(args),
        out_specs=[VMEM] * len(outs),
        scratch_shapes=list(scratch),
        compiler_params=pltpu.CompilerParams(vmem_limit_bytes=48 * 1024 * 1024),
        cost_estimate=pl.CostEstimate(flops=flops, bytes_accessed=moved, transcendentals=0),
    )(*args)


def moves(count_x, count_y, by_x, by_y):
    pairs = []
    for x in range(count_x):
        for y in range(count_y):
            to_x, to_y = x + by_x, y + by_y
            if 0 <= to_x < count_x and 0 <= to_y < count_y:
                pairs.append((x * count_y + y, to_x * count_y + to_y))
    return pairs


def exchange(slots, devices):
    groups, rows, lanes = slots.shape
    per = devices // groups
    if per > 1:
        slots = slots.reshape(groups, rows, per, lanes // per).transpose(0, 2, 1, 3)
        slots = slots.reshape(devices, rows, lanes // per)
    slots = lax.all_to_all(slots, ("gx", "gy"), split_axis=0, concat_axis=0, tiled=True)
    if per > 1:
        slots = slots.reshape(groups, per, rows, lanes // per).transpose(0, 2, 1, 3)
        slots = slots.reshape(groups, rows, lanes)
    return slots


def per_device(
    velocity, stress, lame_lambda, lame_mu, node_mass, displacement,
    seg_elem, seg_bucket, slave_points, candidates,
):
    count_x = lax.axis_size("gx")
    count_y = lax.axis_size("gy")
    devices = count_x * count_y
    _, size_x, size_y, size_z = velocity.shape
    seg_count = seg_elem.shape[0]
    capacity = 2 * seg_count // devices
    slots = devices * capacity
    groups = slots // LANES
    axes = ("gx", "gy")

    def ghosts(own):
        return (
            lax.ppermute(own[:, 0], axes, moves(count_x, count_y, -1, 0)),
            lax.ppermute(own[:, :, 0], axes, moves(count_x, count_y, 0, -1)),
            lax.ppermute(own[:, 0, 0], axes, moves(count_x, count_y, -1, -1)),
        )

    disp_ghosts = ghosts(displacement)
    vel_ghosts = ghosts(velocity)
    (index,) = call(
        functools.partial(index_kernel, devices, capacity, size_z),
        [((8, seg_count), jnp.int32)],
        seg_elem.reshape(1, seg_count),
        seg_bucket.reshape(1, seg_count),
        flops=4_000_000_000,
    )
    chunk = min(512, seg_count)
    (outgoing,) = call(
        functools.partial(geometry_kernel, chunk),
        [((groups, 8, LANES), F32)],
        displacement, *disp_ghosts, index,
        scratch=[pltpu.VMEM((6, size_x, size_y, size_z), F32), pltpu.VMEM((8, chunk), F32)],
        flops=4_000_000_000,
    )
    arrived = exchange(outgoing, devices)
    plane = (3, size_y, size_z)
    planes = [
        (velocity.shape, F32), (plane, F32), ((3, size_x, size_z), F32), ((3, size_z), F32)
    ]
    new_stress, *forces = call(
        stress_kernel,
        [(stress.shape, F32)] + planes,
        velocity, *vel_ghosts, stress, lame_lambda, lame_mu,
        flops=8_000_000_000,
    )
    slave_force, reaction = call(
        contact_kernel,
        [(slave_points.shape, F32), ((groups, 8, LANES), F32)],
        arrived, slave_points, candidates,
        flops=2_000_000_000,
    )
    returned = exchange(reaction, devices)
    force, force_x, force_y, force_c = call(
        functools.partial(nodes_kernel, chunk), planes, returned, index, *forces,
        flops=4_000_000_000,
    )
    from_x = lax.ppermute(force_x, axes, moves(count_x, count_y, 1, 0))
    from_y = lax.ppermute(force_y, axes, moves(count_x, count_y, 0, 1))
    from_c = lax.ppermute(force_c, axes, moves(count_x, count_y, 1, 1))
    (acceleration,) = call(
        final_kernel, [(velocity.shape, F32)], force, from_x, from_y, from_c, node_mass
    )
    return (new_stress, acceleration, slave_force)


def solution(mesh):
    grid = P(None, "gx", "gy", None)
    cells = P("gx", "gy", None)
    return jax.shard_map(
        per_device,
        mesh=mesh,
        in_specs=(
            grid, grid, cells, cells, cells, grid,
            P(("gx", "gy")), P(("gx", "gy"), None), P(None, ("gx", "gy")), P(None, ("gx", "gy")),
        ),
        out_specs=(grid, grid, P(None, ("gx", "gy"))),
        check_vma=False,
    )
```

```python
import functools

import jax
import jax.numpy as jnp
from jax import lax
from jax.experimental import pallas as pl
from jax.experimental.pallas import tpu as pltpu
from jax.sharding import PartitionSpec as P

time_step = 0.1
penalty = 10.0
LANES = 128
F32 = jnp.float32
BF16 = jnp.bfloat16
VMEM = pl.BlockSpec(memory_space=pltpu.VMEM)
NN = (((1,), (0,)), ((), ()))
NT = (((1,), (1,)), ((), ()))


def split_index(value, size):
    if size & (size - 1) == 0:
        return value >> (size.bit_length() - 1), value & (size - 1)
    return value // size, value % size


def two_terms(value):
    high = value.astype(BF16)
    return high, (value - high.astype(F32)).astype(BF16)


def dot(left, right, dims):
    return lax.dot_general(left, right, dims, preferred_element_type=F32)


def one_hot(row, count):
    return lax.broadcasted_iota(jnp.int32, (count, row.shape[1]), 0) == row


def next_row(tile, last):
    rows = tile.shape[0]
    rolled = pltpu.roll(tile, rows - 1, 0)
    return jnp.where(lax.broadcasted_iota(jnp.int32, tile.shape, 0) == rows - 1, last, rolled)


def previous_row(tile):
    rolled = pltpu.roll(tile, 1, 0)
    return jnp.where(lax.broadcasted_iota(jnp.int32, tile.shape, 0) == 0, 0.0, rolled)


def next_lane(tile):
    lanes = tile.shape[1]
    rolled = pltpu.roll(tile, lanes - 1, 1)
    return jnp.where(lax.broadcasted_iota(jnp.int32, tile.shape, 1) == lanes - 1, 0.0, rolled)


def previous_lane(tile):
    rolled = pltpu.roll(tile, 1, 1)
    return jnp.where(lax.broadcasted_iota(jnp.int32, tile.shape, 1) == 0, 0.0, rolled)


def index_kernel(devices, capacity, size_z, elem, bucket, out):
    count = elem.shape[1]
    row, depth = split_index(elem[...], size_z)
    out[0:1] = depth + 1
    out[1:2] = row
    tri = (
        lax.broadcasted_iota(jnp.int32, (LANES, LANES), 0)
        <= lax.broadcasted_iota(jnp.int32, (LANES, LANES), 1)
    ).astype(F32).astype(BF16)
    carry = jnp.zeros((devices, 1), F32)
    for start in range(0, count, LANES):
        here = bucket[:, start : start + LANES]
        hot = one_hot(here, devices).astype(F32)
        running = dot(hot.astype(BF16), tri, NN)
        rank = jnp.sum(hot * (running + carry), axis=0, keepdims=True) - 1.0
        carry = carry + running[:, LANES - 1 : LANES]
        target = here * capacity + rank.astype(jnp.int32)
        high, low = split_index(target, LANES)
        out[2:3, start : start + LANES] = high
        out[3:4, start : start + LANES] = low
    out[4:8] = jnp.zeros((4, count), jnp.int32)


def spread(values, high, groups):
    rows, lanes = values.shape
    which = lax.broadcasted_iota(jnp.int32, (groups, rows, lanes), 0)
    kept = jnp.where(which == high[None], values[None], 0.0)
    return kept.reshape(groups * rows, lanes)


def picked(table, high, groups):
    rows = table.shape[0] // groups
    lanes = table.shape[1]
    total = jnp.zeros((rows, lanes), F32)
    for group in range(groups):
        total = jnp.where(high == group, table[group * rows : (group + 1) * rows], total)
    return total


def geometry(chunk, own, ghost_x, ghost_y, ghost_c, index, groups, faces, payload):
    size_x, size_y, size_z = own.shape[1:]
    count = index.shape[1]

    def plane(comp, i):
        return own[comp, i] if i < size_x else ghost_x[comp]

    def last_row(comp, i):
        return ghost_y[comp, i : i + 1] if i < size_x else ghost_c[comp : comp + 1]

    for i in range(size_x):
        p, q = [], []
        for comp in range(3):
            low, high = plane(comp, i), plane(comp, i + 1)
            low_next = next_row(low, last_row(comp, i))
            high_next = next_row(high, last_row(comp, i + 1))
            faces[comp, i] = 0.25 * ((low + high) + (low_next + high_next))
            p.append(high_next - low)
            q.append(low_next - high)
        faces[3, i] = 0.5 * ((1.0 + p[1]) * q[2] - p[2] * (1.0 + q[1]))
        faces[4, i] = 0.5 * (p[2] * (q[0] - 1.0) - (1.0 + p[0]) * q[2])
        faces[5, i] = 0.5 * (p[0] + p[1] + q[1] - q[0] + p[0] * q[1] - p[1] * q[0])
    rows = size_x * size_y
    high, low = two_terms(faces[...].reshape(6 * rows, size_z))
    total = jnp.zeros((groups * 8, LANES), F32)
    payload[6:7] = jnp.ones((1, chunk), F32)
    payload[7:8] = jnp.zeros((1, chunk), F32)
    for start in range(0, count, chunk):
        here = slice(start, start + chunk)
        hot = one_hot(index[0:1, here], size_z).astype(F32).astype(BF16)
        near = dot(high, hot, NN) + dot(low, hot, NN)
        hot_row = one_hot(index[1:2, here], rows)
        for comp in range(6):
            payload[comp : comp + 1] = jnp.sum(
                jnp.where(hot_row, near[comp * rows : (comp + 1) * rows], 0.0), axis=0, keepdims=True
            )
        slot = index[2:3, here]
        hot_low = one_hot(index[3:4, here], LANES).astype(F32).astype(BF16)
        values = payload[...]
        part = values.astype(BF16).astype(F32)
        total += dot(spread(part, slot, groups).astype(BF16), hot_low, NT)
        total += dot(spread(values - part, slot, groups).astype(BF16), hot_low, NT)
    return total


def stress_kernel(
    own, ghost_x, ghost_y, ghost_c, stress, lame_lambda, lame_mu,
    new_stress, force, force_x, force_y, force_c,
):
    size_x = own.shape[1]
    size_y = own.shape[2]

    def plane(comp, i):
        tile = own[comp, i] if i < size_x else ghost_x[comp]
        last = ghost_y[comp, i : i + 1] if i < size_x else ghost_c[comp : comp + 1]
        after = next_row(tile, last)
        both, change = tile + after, after - tile
        return both + next_lane(both), change + next_lane(change), next_lane(both) - both

    low = [plane(comp, 0) for comp in range(3)]
    carry = None
    for i in range(size_x):
        high = [plane(comp, i + 1) for comp in range(3)]
        grad_x = [high[c][0] - low[c][0] for c in range(3)]
        grad_y = [high[c][1] + low[c][1] for c in range(3)]
        grad_z = [high[c][2] + low[c][2] for c in range(3)]
        low = high
        shear = (0.5 * time_step) * lame_mu[i]
        volume = (0.25 * time_step) * lame_lambda[i] * (grad_x[0] + grad_y[1] + grad_z[2])
        s_xx = stress[0, i] + (volume + shear * grad_x[0])
        s_yy = stress[1, i] + (volume + shear * grad_y[1])
        s_zz = stress[2, i] + (volume + shear * grad_z[2])
        half = 0.5 * shear
        s_yz = stress[3, i] + half * (grad_z[1] + grad_y[2])
        s_xz = stress[4, i] + half * (grad_z[0] + grad_x[2])
        s_xy = stress[5, i] + half * (grad_y[0] + grad_x[1])
        for number, value in enumerate((s_xx, s_yy, s_zz, s_yz, s_xz, s_xy)):
            new_stress[number, i] = value
        tensor = ((s_xx, s_xy, s_xz), (s_xy, s_yy, s_yz), (s_xz, s_yz, s_zz))
        later = []
        for comp in range(3):
            first, second, third = (-0.25 * t for t in tensor[comp])
            first = first + previous_lane(first)
            second = second + previous_lane(second)
            third = previous_lane(third) - third
            near_plus, near_minus = third - second + first, third - second - first
            far_plus, far_minus = third + second + first, third + second - first
            plus = near_plus + previous_row(far_plus)
            minus = near_minus + previous_row(far_minus)
            plus_end = far_plus[size_y - 1 : size_y]
            minus_end = far_minus[size_y - 1 : size_y]
            if carry is not None:
                minus = minus + carry[comp][0]
                minus_end = minus_end + carry[comp][1]
            force[comp, i] = minus
            force_y[comp, i : i + 1] = minus_end
            later.append((plus, plus_end))
        carry = later
    for comp in range(3):
        force_x[comp] = carry[comp][0]
        force_c[comp : comp + 1] = carry[comp][1]


def contact(arrived, points, candidates, slave_force):
    groups = arrived.shape[0] // 8
    lanes = points.shape[1]
    high, low = two_terms(arrived)
    total = jnp.zeros((groups * 8, LANES), F32)
    pushed = [jnp.zeros((1, lanes), F32) for _ in range(3)]
    eight = lax.broadcasted_iota(jnp.int32, (8, lanes), 0)
    for k in range(candidates.shape[0]):
        slot, place = split_index(candidates[k : k + 1], LANES)
        hot = one_hot(place, LANES).astype(F32).astype(BF16)
        near = picked(dot(high, hot, NN) + dot(low, hot, NN), slot, groups)
        rows = [near[r : r + 1] for r in range(7)]
        filled = rows[6]
        offset = (0.5, 0.5, 1.0)
        area = (rows[3], rows[4], rows[5] + filled)
        gap = jnp.zeros((1, lanes), F32)
        for comp in range(3):
            gap = gap + area[comp] * (points[comp : comp + 1] - (rows[comp] + offset[comp] * filled))
        scale = penalty * jnp.maximum(-gap, 0.0)
        values = jnp.zeros((8, lanes), F32)
        for comp in range(3):
            push = scale * area[comp]
            pushed[comp] = pushed[comp] + push
            values = jnp.where(eight == comp, -push, values)
        part = values.astype(BF16).astype(F32)
        total += dot(spread(part, slot, groups).astype(BF16), hot, NT)
        total += dot(spread(values - part, slot, groups).astype(BF16), hot, NT)
    for comp in range(3):
        slave_force[comp : comp + 1] = pushed[comp]
    return total


def nodes_kernel(chunk, returned, index, force, force_x, force_y, force_c):
    size_x, size_y, size_z = force.shape[1:]
    groups = returned.shape[0] // 8
    count = index.shape[1]
    rows = size_x * size_y
    high, low = two_terms(returned)
    total = jnp.zeros((3 * rows, size_z), F32)
    for start in range(0, count, chunk):
        here = slice(start, start + chunk)
        hot_low = one_hot(index[3:4, here], LANES).astype(F32).astype(BF16)
        near = picked(dot(high, hot_low, NN) + dot(low, hot_low, NN), index[2:3, here], groups)
        quarter = 0.25 * near
        part = quarter.astype(BF16).astype(F32)
        rest = quarter - part
        hot_row = one_hot(index[1:2, here], rows)
        hot = one_hot(index[0:1, here], size_z).astype(F32).astype(BF16)
        for values in (part, rest):
            left = jnp.concatenate(
                [jnp.where(hot_row, values[c : c + 1], 0.0) for c in range(3)], 0
            ).astype(BF16)
            total += dot(left, hot, NT)
    for comp in range(3):
        before = None
        for i in range(size_x):
            at = (comp * size_x + i) * size_y
            tile = total[at : at + size_y]
            both = tile + previous_row(tile)
            end = tile[size_y - 1 : size_y]
            value, value_end = both, end
            if before is not None:
                value, value_end = both + before[0], end + before[1]
            force[comp, i] = force[comp, i] + value
            force_y[comp, i : i + 1] = force_y[comp, i : i + 1] + value_end
            before = (both, end)
        force_x[comp] = force_x[comp] + before[0]
        force_c[comp : comp + 1] = force_c[comp : comp + 1] + before[1]


def final_kernel(force, from_x, from_y, from_c, mass):
    size_x = force.shape[1]
    first = lax.broadcasted_iota(jnp.int32, force.shape[2:], 0) == 0
    for i in range(size_x):
        inverse = 1.0 / mass[i]
        for comp in range(3):
            end = from_y[comp, i : i + 1]
            value = force[comp, i]
            if i == 0:
                end = end + from_c[comp : comp + 1]
                value = value + from_x[comp]
            force[comp, i] = (value + jnp.where(first, end, 0.0)) * inverse


def to_messages(total, messages):
    devices, rows, capacity = messages.shape
    per = LANES // capacity
    if per == 1:
        messages[...] = total.reshape(messages.shape)
        return
    for device in range(devices):
        group, part = device // per, device % per
        messages[device] = total[
            group * rows : (group + 1) * rows, part * capacity : (part + 1) * capacity
        ]


def from_messages(messages):
    devices, rows, capacity = messages.shape
    per = LANES // capacity
    if per == 1:
        return messages[...].reshape(devices * rows, LANES)
    return jnp.concatenate(
        [
            jnp.concatenate([messages[group * per + part] for part in range(per)], 1)
            for group in range(devices // per)
        ],
        0,
    )


def fused_kernel(
    count_x, count_y, chunk,
    disp, vel, stress, lame_lambda, lame_mu, mass, elem, bucket, points, candidates,
    new_stress, acceleration, slave_force,
    index, faces, payload,
    disp_x, disp_y, disp_c, vel_x, vel_y, vel_c,
    disp_row, disp_edge, vel_row, vel_edge,
    slots_out, slots_in, back_out, back_in,
    force_x, force_y, force_c, from_x, from_y, from_c,
    halo_send, halo_recv, force_send, force_recv, slot_send, slot_recv,
):
    devices = count_x * count_y
    _, size_x, size_y, size_z = vel.shape
    capacity = slots_out.shape[2]
    at_x, at_y = lax.axis_index("gx"), lax.axis_index("gy")
    me = at_x * count_y + at_y

    def peer(step):
        other = lax.rem(me + step, devices)
        return other, (lax.div(other, count_y), lax.rem(other, count_y))

    def remote(src, dst, send, recv, to):
        return pltpu.make_async_remote_copy(
            src_ref=src, dst_ref=dst, send_sem=send, recv_sem=recv,
            device_id=to, device_id_type=pl.DeviceIdType.MESH,
        )

    barrier = pltpu.get_barrier_semaphore()

    @pl.loop(1, devices)
    def _(step):
        pl.semaphore_signal(
            barrier, inc=1, device_id=peer(step)[1], device_id_type=pl.DeviceIdType.MESH
        )

    for own, row, edge in ((disp, disp_row, disp_edge), (vel, vel_row, vel_edge)):
        for comp in range(3):
            for i in range(size_x):
                row[comp, i : i + 1] = own[comp, i, 0:1]
            edge[comp : comp + 1] = own[comp, 0, 0:1]
    pl.semaphore_wait(barrier, devices - 1)

    down_x, down_y = at_x > 0, at_y > 0
    up_x, up_y = at_x < count_x - 1, at_y < count_y - 1
    below = ((at_x - 1, at_y), (at_x, at_y - 1), (at_x - 1, at_y - 1))
    above = ((at_x + 1, at_y), (at_x, at_y + 1), (at_x + 1, at_y + 1))
    has_below = (down_x, down_y, jnp.logical_and(down_x, down_y))
    has_above = (up_x, up_y, jnp.logical_and(up_x, up_y))

    halo_in = (
        (disp.at[:, 0], disp_x), (disp_row, disp_y), (disp_edge, disp_c),
        (vel.at[:, 0], vel_x), (vel_row, vel_y), (vel_edge, vel_c),
    )
    halo_out = ((force_x, from_x), (force_y, from_y), (force_c, from_c))

    def start(copies, sends, recvs, to, allowed):
        for n, (src, dst) in enumerate(copies):
            @pl.when(allowed[n % 3])
            def _():
                remote(src, dst, sends.at[n], recvs.at[n], to[n % 3]).start()

    def finish(copies, sends, recvs, to, sent, got, which):
        for n in which:
            src, dst = copies[n]

            @pl.when(got[n % 3])
            def _():
                remote(src, dst, sends.at[n], recvs.at[n], to[n % 3]).wait_recv()

            @pl.when(sent[n % 3])
            def _():
                remote(src, dst, sends.at[n], recvs.at[n], to[n % 3]).wait_send()

            @pl.when(jnp.logical_not(got[n % 3]))
            def _():
                dst[...] = jnp.zeros(dst.shape, F32)

    def scatter(outgoing, incoming, n):
        @pl.loop(1, devices)
        def _(step):
            other, to = peer(step)
            remote(
                outgoing.at[other], incoming.at[me], slot_send.at[n], slot_recv.at[n], to
            ).start()

        incoming[me] = outgoing[me]

    def gather(outgoing, incoming, n):
        most = pl.ds(0, devices - 1)
        whole = remote(
            outgoing.at[most], incoming.at[most], slot_send.at[n], slot_recv.at[n], peer(1)[1]
        )
        whole.wait_send()
        whole.wait_recv()

    start(halo_in, halo_send, halo_recv, below, has_below)
    index_kernel(devices, capacity, size_z, elem, bucket, index)
    finish(halo_in, halo_send, halo_recv, below, has_below, has_above, (0, 1, 2))
    to_messages(
        geometry(chunk, disp, disp_x, disp_y, disp_c, index, devices * capacity // LANES, faces, payload),
        slots_out,
    )
    scatter(slots_out, slots_in, 0)
    finish(halo_in, halo_send, halo_recv, below, has_below, has_above, (3, 4, 5))
    stress_kernel(
        vel, vel_x, vel_y, vel_c, stress, lame_lambda, lame_mu,
        new_stress, acceleration, force_x, force_y, force_c,
    )
    gather(slots_out, slots_in, 0)
    to_messages(contact(from_messages(slots_in), points, candidates, slave_force), back_out)
    scatter(back_out, back_in, 1)
    gather(back_out, back_in, 1)
    nodes_kernel(chunk, from_messages(back_in), index, acceleration, force_x, force_y, force_c)
    start(halo_out, force_send, force_recv, above, has_above)
    finish(halo_out, force_send, force_recv, above, has_above, has_below, (0, 1, 2))
    final_kernel(acceleration, from_x, from_y, from_c, mass)


def per_device(
    velocity, stress, lame_lambda, lame_mu, node_mass, displacement,
    seg_elem, seg_bucket, slave_points, candidates,
):
    count_x = lax.axis_size("gx")
    count_y = lax.axis_size("gy")
    devices = count_x * count_y
    _, size_x, size_y, size_z = velocity.shape
    seg_count = seg_elem.shape[0]
    capacity = 2 * seg_count // devices
    chunk = min(512, seg_count)
    args = (
        displacement, velocity, stress, lame_lambda, lame_mu, node_mass,
        seg_elem.reshape(1, seg_count), seg_bucket.reshape(1, seg_count),
        slave_points, candidates,
    )
    outs = (stress.shape, velocity.shape, slave_points.shape)
    side_x, side_y, side_c = (3, size_y, size_z), (3, size_x, size_z), (3, size_z)
    message = (devices, 8, capacity)
    shapes = (
        [(6, size_x, size_y, size_z), (8, chunk)]
        + [side_x, side_y, side_c] * 2
        + [side_y, side_c] * 2
        + [message] * 4
        + [side_x, side_y, side_c] * 2
    )
    new_stress, acceleration, slave_force = pl.pallas_call(
        functools.partial(fused_kernel, count_x, count_y, chunk),
        out_shape=[jax.ShapeDtypeStruct(s, F32) for s in outs],
        in_specs=[VMEM] * len(args),
        out_specs=[VMEM] * len(outs),
        scratch_shapes=[pltpu.VMEM((8, seg_count), jnp.int32)]
        + [pltpu.VMEM(s, F32) for s in shapes]
        + [pltpu.SemaphoreType.DMA((n,)) for n in (6, 6, 3, 3, 2, 2)],
        compiler_params=pltpu.CompilerParams(
            collective_id=0, has_side_effects=True, vmem_limit_bytes=48 * 1024 * 1024
        ),
    )(*args)
    return (new_stress, acceleration, slave_force)


def solution(mesh):
    grid = P(None, "gx", "gy", None)
    cells = P("gx", "gy", None)
    return jax.shard_map(
        per_device,
        mesh=mesh,
        in_specs=(
            grid, grid, cells, cells, cells, grid,
            P(("gx", "gy")), P(("gx", "gy"), None), P(None, ("gx", "gy")), P(None, ("gx", "gy")),
        ),
        out_specs=(grid, grid, P(None, ("gx", "gy"))),
        check_vma=False,
    )
```

```python
import functools

import jax
import jax.numpy as jnp
from jax import lax
from jax.experimental import pallas as pl
from jax.experimental.pallas import tpu as pltpu
from jax.sharding import PartitionSpec as P

time_step = 0.1
penalty = 10.0
LANES = 128
F32 = jnp.float32
BF16 = jnp.bfloat16
VMEM = pl.BlockSpec(memory_space=pltpu.VMEM)
HBM = pl.BlockSpec(memory_space=pltpu.HBM)
NN = (((1,), (0,)), ((), ()))
NT = (((1,), (1,)), ((), ()))


def split_index(value, size):
    if size & (size - 1) == 0:
        return value >> (size.bit_length() - 1), value & (size - 1)
    return value // size, value % size


def two_terms(value):
    high = value.astype(BF16)
    return high, (value - high.astype(F32)).astype(BF16)


def dot(left, right, dims):
    return lax.dot_general(left, right, dims, preferred_element_type=F32)


def one_hot(row, count):
    return lax.broadcasted_iota(jnp.int32, (count, row.shape[1]), 0) == row


def next_row(tile, last):
    rows = tile.shape[0]
    rolled = pltpu.roll(tile, rows - 1, 0)
    return jnp.where(lax.broadcasted_iota(jnp.int32, tile.shape, 0) == rows - 1, last, rolled)


def previous_row(tile):
    rolled = pltpu.roll(tile, 1, 0)
    return jnp.where(lax.broadcasted_iota(jnp.int32, tile.shape, 0) == 0, 0.0, rolled)


def next_lane(tile):
    lanes = tile.shape[1]
    rolled = pltpu.roll(tile, lanes - 1, 1)
    return jnp.where(lax.broadcasted_iota(jnp.int32, tile.shape, 1) == lanes - 1, 0.0, rolled)


def previous_lane(tile):
    rolled = pltpu.roll(tile, 1, 1)
    return jnp.where(lax.broadcasted_iota(jnp.int32, tile.shape, 1) == 0, 0.0, rolled)


def index_kernel(devices, capacity, size_x, size_y, size_z, elem, bucket, out):
    count = elem.shape[1]
    row, depth = split_index(elem[...], size_z)
    cell_i, cell_j = split_index(row, size_y)
    ends = cell_j == size_y - 1
    out[0:1] = depth + 1
    out[1:2] = row
    out[4:5] = jnp.where(ends, -1, row)
    out[5:6] = row - (size_x - 1) * size_y
    out[6:7] = jnp.where(ends & (cell_i < size_x - 1), cell_i, -1)
    out[7:8] = jnp.zeros((1, count), jnp.int32)
    tri = (
        lax.broadcasted_iota(jnp.int32, (LANES, LANES), 0)
        <= lax.broadcasted_iota(jnp.int32, (LANES, LANES), 1)
    ).astype(F32).astype(BF16)
    carry = jnp.zeros((devices, 1), F32)
    for start in range(0, count, LANES):
        here = bucket[:, start : start + LANES]
        hot = one_hot(here, devices).astype(F32)
        running = dot(hot.astype(BF16), tri, NN)
        rank = jnp.sum(hot * (running + carry), axis=0, keepdims=True) - 1.0
        carry = carry + running[:, LANES - 1 : LANES]
        target = here * capacity + rank.astype(jnp.int32)
        high, low = split_index(target, LANES)
        out[2:3, start : start + LANES] = high
        out[3:4, start : start + LANES] = low


def spread(values, high, groups):
    rows, lanes = values.shape
    which = lax.broadcasted_iota(jnp.int32, (groups, rows, lanes), 0)
    kept = jnp.where(which == high[None], values[None], 0.0)
    return kept.reshape(groups * rows, lanes)


def picked(table, high, groups):
    rows = table.shape[0] // groups
    lanes = table.shape[1]
    total = jnp.zeros((rows, lanes), F32)
    for group in range(groups):
        total = jnp.where(high == group, table[group * rows : (group + 1) * rows], total)
    return total


def face_values(low, high, low_next, high_next):
    mean = [0.25 * ((low[c] + high[c]) + (low_next[c] + high_next[c])) for c in range(3)]
    p = [high_next[c] - low[c] for c in range(3)]
    q = [low_next[c] - high[c] for c in range(3)]
    return mean + [
        0.5 * ((1.0 + p[1]) * q[2] - p[2] * (1.0 + q[1])),
        0.5 * (p[2] * (q[0] - 1.0) - (1.0 + p[0]) * q[2]),
        0.5 * (p[0] + p[1] + q[1] - q[0] + p[0] * q[1] - p[1] * q[0]),
    ]


def chosen(table, hot_row, at):
    rows = hot_row.shape[0]
    return jnp.sum(jnp.where(hot_row, table[at : at + rows], 0.0), axis=0, keepdims=True)


def bf16_hot(row, count):
    return one_hot(row, count).astype(F32).astype(BF16)


def inner_faces(chunk, own, index, faces, payload, hot_depth, hot_low):
    size_x, size_y, size_z = own.shape[1:]
    count = index.shape[1]
    for i in range(size_x - 1):
        low = [own[c, i] for c in range(3)]
        high = [own[c, i + 1] for c in range(3)]
        after = [pltpu.roll(t, size_y - 1, 0) for t in low]
        high_after = [pltpu.roll(t, size_y - 1, 0) for t in high]
        for number, value in enumerate(face_values(low, high, after, high_after)):
            faces[number, i] = value
    rows = (size_x - 1) * size_y
    high, low = two_terms(faces[...].reshape(6 * rows, size_z))
    for start in range(0, count, chunk):
        here = slice(start, start + chunk)
        hot = bf16_hot(index[0:1, here], size_z)
        hot_depth[:, here] = hot
        hot_low[:, here] = bf16_hot(index[3:4, here], LANES)
        near = dot(high, hot, NN) + dot(low, hot, NN)
        hot_row = one_hot(index[4:5, here], rows)
        for comp in range(6):
            payload[comp : comp + 1, here] = chosen(near, hot_row, comp * rows)
    payload[6:7] = jnp.ones((1, count), F32)
    payload[7:8] = jnp.zeros((1, count), F32)


def all_faces(
    chunk, own, own_last, ghost_x, ghost_y, ghost_c, index, groups, edges, payload, hot_depth, hot_low
):
    size_x, size_y, size_z = own.shape[1:]
    count = index.shape[1]
    low = [own[c, size_x - 1] for c in range(3)]
    high = [ghost_x[c] for c in range(3)]
    after = [next_row(low[c], ghost_y[c, size_x - 1 : size_x]) for c in range(3)]
    high_after = [next_row(high[c], ghost_c[c : c + 1]) for c in range(3)]
    at = 0
    for value in face_values(low, high, after, high_after):
        edges[at : at + size_y] = value
        at += size_y
    low = [own_last[c] for c in range(3)]
    after = [ghost_y[c] for c in range(3)]
    high = [pltpu.roll(t, size_x - 1, 0) for t in low]
    high_after = [pltpu.roll(t, size_x - 1, 0) for t in after]
    for value in face_values(low, high, after, high_after):
        edges[at : at + size_x] = value
        at += size_x
    high, low = two_terms(edges[...])
    total = jnp.zeros((groups * 8, LANES), F32)
    for start in range(0, count, chunk):
        here = slice(start, start + chunk)
        hot = hot_depth[:, here]
        near = dot(high, hot, NN) + dot(low, hot, NN)
        hot_x = one_hot(index[5:6, here], size_y)
        hot_y = one_hot(index[6:7, here], size_x)
        for comp in range(6):
            payload[comp : comp + 1, here] += chosen(near, hot_x, comp * size_y) + chosen(
                near, hot_y, 6 * size_y + comp * size_x
            )
        slot = index[2:3, here]
        values = payload[:, here]
        part = values.astype(BF16).astype(F32)
        total += dot(spread(part, slot, groups).astype(BF16), hot_low[:, here], NT)
        total += dot(spread(values - part, slot, groups).astype(BF16), hot_low[:, here], NT)
    return total


def stress_kernel(
    own, ghost_x, ghost_y, ghost_c, stress, lame_lambda, lame_mu,
    new_stress, force, force_x, force_y, force_c,
):
    size_x = own.shape[1]
    size_y = own.shape[2]

    def plane(comp, i):
        tile = own[comp, i] if i < size_x else ghost_x[comp]
        last = ghost_y[comp, i : i + 1] if i < size_x else ghost_c[comp : comp + 1]
        after = next_row(tile, last)
        both, change = tile + after, after - tile
        return both + next_lane(both), change + next_lane(change), next_lane(both) - both

    low = [plane(comp, 0) for comp in range(3)]
    carry = None
    for i in range(size_x):
        high = [plane(comp, i + 1) for comp in range(3)]
        grad_x = [high[c][0] - low[c][0] for c in range(3)]
        grad_y = [high[c][1] + low[c][1] for c in range(3)]
        grad_z = [high[c][2] + low[c][2] for c in range(3)]
        low = high
        shear = (0.5 * time_step) * lame_mu[i]
        volume = (0.25 * time_step) * lame_lambda[i] * (grad_x[0] + grad_y[1] + grad_z[2])
        s_xx = stress[0, i] + (volume + shear * grad_x[0])
        s_yy = stress[1, i] + (volume + shear * grad_y[1])
        s_zz = stress[2, i] + (volume + shear * grad_z[2])
        half = 0.5 * shear
        s_yz = stress[3, i] + half * (grad_z[1] + grad_y[2])
        s_xz = stress[4, i] + half * (grad_z[0] + grad_x[2])
        s_xy = stress[5, i] + half * (grad_y[0] + grad_x[1])
        for number, value in enumerate((s_xx, s_yy, s_zz, s_yz, s_xz, s_xy)):
            new_stress[number, i] = value
        tensor = ((s_xx, s_xy, s_xz), (s_xy, s_yy, s_yz), (s_xz, s_yz, s_zz))
        later = []
        for comp in range(3):
            first, second, third = (-0.25 * t for t in tensor[comp])
            first = first + previous_lane(first)
            second = second + previous_lane(second)
            third = previous_lane(third) - third
            near_plus, near_minus = third - second + first, third - second - first
            far_plus, far_minus = third + second + first, third + second - first
            plus = near_plus + previous_row(far_plus)
            minus = near_minus + previous_row(far_minus)
            plus_end = far_plus[size_y - 1 : size_y]
            minus_end = far_minus[size_y - 1 : size_y]
            if carry is not None:
                minus = minus + carry[comp][0]
                minus_end = minus_end + carry[comp][1]
            force[comp, i] = minus
            force_y[comp, i : i + 1] = minus_end
            later.append((plus, plus_end))
        carry = later
    for comp in range(3):
        force_x[comp] = carry[comp][0]
        force_c[comp : comp + 1] = carry[comp][1]


def contact(arrived, points, candidates, hot_slot, slave_force):
    groups = arrived.shape[0] // 8
    lanes = points.shape[1]
    high, low = two_terms(arrived)
    total = jnp.zeros((groups * 8, LANES), F32)
    pushed = [jnp.zeros((1, lanes), F32) for _ in range(3)]
    eight = lax.broadcasted_iota(jnp.int32, (8, lanes), 0)
    for k in range(candidates.shape[0]):
        slot = split_index(candidates[k : k + 1], LANES)[0]
        hot = hot_slot[k]
        near = picked(dot(high, hot, NN) + dot(low, hot, NN), slot, groups)
        rows = [near[r : r + 1] for r in range(7)]
        filled = rows[6]
        offset = (0.5, 0.5, 1.0)
        area = (rows[3], rows[4], rows[5] + filled)
        gap = jnp.zeros((1, lanes), F32)
        for comp in range(3):
            gap = gap + area[comp] * (points[comp : comp + 1] - (rows[comp] + offset[comp] * filled))
        scale = penalty * jnp.maximum(-gap, 0.0)
        values = jnp.zeros((8, lanes), F32)
        for comp in range(3):
            push = scale * area[comp]
            pushed[comp] = pushed[comp] + push
            values = jnp.where(eight == comp, -push, values)
        part = values.astype(BF16).astype(F32)
        total += dot(spread(part, slot, groups).astype(BF16), hot, NT)
        total += dot(spread(values - part, slot, groups).astype(BF16), hot, NT)
    for comp in range(3):
        slave_force[comp : comp + 1] = pushed[comp]
    return total


def nodes_kernel(
    chunk, returned, index, hot_depth, hot_low, force, force_x, force_y, force_c
):
    size_x, size_y, size_z = force.shape[1:]
    groups = returned.shape[0] // 8
    count = index.shape[1]
    rows = size_x * size_y
    high, low = two_terms(returned)
    total = jnp.zeros((3 * rows, size_z), F32)
    for start in range(0, count, chunk):
        here = slice(start, start + chunk)
        place = hot_low[:, here]
        near = picked(dot(high, place, NN) + dot(low, place, NN), index[2:3, here], groups)
        quarter = 0.25 * near
        part = quarter.astype(BF16).astype(F32)
        rest = quarter - part
        hot_row = one_hot(index[1:2, here], rows)
        hot = hot_depth[:, here]
        for values in (part, rest):
            left = jnp.concatenate(
                [jnp.where(hot_row, values[c : c + 1], 0.0) for c in range(3)], 0
            ).astype(BF16)
            total += dot(left, hot, NT)
    for comp in range(3):
        before = None
        for i in range(size_x):
            at = (comp * size_x + i) * size_y
            tile = total[at : at + size_y]
            both = tile + previous_row(tile)
            end = tile[size_y - 1 : size_y]
            value, value_end = both, end
            if before is not None:
                value, value_end = both + before[0], end + before[1]
            force[comp, i] = force[comp, i] + value
            force_y[comp, i : i + 1] = force_y[comp, i : i + 1] + value_end
            before = (both, end)
        force_x[comp] = force_x[comp] + before[0]
        force_c[comp : comp + 1] = force_c[comp : comp + 1] + before[1]


def final_kernel(
    stress, pushed, force_in, from_x_in, from_y_in, from_c_in, mass_in,
    new_stress, acceleration, slave_force,
    force, from_x, from_y, from_c, mass, result, sems,
):
    copies = [
        pltpu.make_async_copy(src, dst, sems.at[n])
        for n, (src, dst) in enumerate(
            (
                (mass_in, mass), (force_in, force), (from_x_in, from_x), (from_y_in, from_y),
                (from_c_in, from_c), (stress, new_stress), (pushed, slave_force),
                (result, acceleration),
            )
        )
    ]
    for copy in copies[:7]:
        copy.start()
    for copy in copies[:5]:
        copy.wait()
    size_x = force.shape[1]
    first = lax.broadcasted_iota(jnp.int32, force.shape[2:], 0) == 0
    for i in range(size_x):
        inverse = 1.0 / mass[i]
        for comp in range(3):
            end = from_y[comp, i : i + 1]
            value = force[comp, i]
            if i == 0:
                end = end + from_c[comp : comp + 1]
                value = value + from_x[comp]
            result[comp, i] = (value + jnp.where(first, end, 0.0)) * inverse
    copies[7].start()
    for copy in copies[5:]:
        copy.wait()


def to_messages(total, messages):
    devices, rows, capacity = messages.shape
    per = LANES // capacity
    if per == 1:
        messages[...] = total.reshape(messages.shape)
        return
    for device in range(devices):
        group, part = device // per, device % per
        messages[device] = total[
            group * rows : (group + 1) * rows, part * capacity : (part + 1) * capacity
        ]


def from_messages(messages):
    devices, rows, capacity = messages.shape
    per = LANES // capacity
    if per == 1:
        return messages[...].reshape(devices * rows, LANES)
    return jnp.concatenate(
        [
            jnp.concatenate([messages[group * per + part] for part in range(per)], 1)
            for group in range(devices // per)
        ],
        0,
    )


def fused_kernel(
    count_x, count_y, chunk,
    disp_in, elem_in, bucket_in, vel_in, stress_in, lambda_in, mu_in, points_in, candidates_in,
    stress_out, force, slave_force, from_x, from_y, from_c,
    new_stress, disp, elem, bucket, vel, stress, lame_lambda, lame_mu, points, candidates,
    index, hot_depth, hot_low, hot_slot, faces, edges, payload, disp_last,
    disp_x, disp_y, disp_c, vel_x, vel_y, vel_c,
    disp_row, disp_edge, vel_row, vel_edge,
    slots_out, slots_in, back_out, back_in,
    force_x, force_y, force_c,
    load_sems, store_sem, halo_send, halo_recv, force_send, force_recv, slot_send, slot_recv,
):
    devices = count_x * count_y
    _, size_x, size_y, size_z = vel.shape
    capacity = slots_out.shape[2]
    groups = devices * capacity // LANES
    kept = (7, 3)
    at_x, at_y = lax.axis_index("gx"), lax.axis_index("gy")
    me = at_x * count_y + at_y

    def peer(step):
        other = lax.rem(me + step, devices)
        return other, (lax.div(other, count_y), lax.rem(other, count_y))

    def remote(src, dst, send, recv, to):
        return pltpu.make_async_remote_copy(
            src_ref=src, dst_ref=dst, send_sem=send, recv_sem=recv,
            device_id=to, device_id_type=pl.DeviceIdType.MESH,
        )

    loads = [
        pltpu.make_async_copy(src, dst, load_sems.at[n])
        for n, (src, dst) in enumerate(
            (
                (disp_in, disp), (elem_in, elem), (bucket_in, bucket), (vel_in, vel),
                (stress_in, stress), (lambda_in, lame_lambda), (mu_in, lame_mu),
                (points_in, points), (candidates_in, candidates),
            )
        )
    ]
    for load in loads:
        load.start()
    barrier = pltpu.get_barrier_semaphore()

    @pl.loop(1, devices)
    def _(step):
        pl.semaphore_signal(
            barrier, inc=1, device_id=peer(step)[1], device_id_type=pl.DeviceIdType.MESH
        )

    def pack(own, row, edge):
        for comp in range(3):
            for i in range(size_x):
                row[comp, i : i + 1] = own[comp, i, 0:1]
            edge[comp : comp + 1] = own[comp, 0, 0:1]

    loads[0].wait()
    pack(disp, disp_row, disp_edge)
    for comp in range(3):
        for i in range(size_x):
            disp_last[comp, i : i + 1] = disp[comp, i, size_y - 1 : size_y]
    pl.semaphore_wait(barrier, devices - 1)

    down_x, down_y = at_x > 0, at_y > 0
    up_x, up_y = at_x < count_x - 1, at_y < count_y - 1
    below = ((at_x - 1, at_y), (at_x, at_y - 1), (at_x - 1, at_y - 1))
    above = ((at_x + 1, at_y), (at_x, at_y + 1), (at_x + 1, at_y + 1))
    has_below = (down_x, down_y, jnp.logical_and(down_x, down_y))
    has_above = (up_x, up_y, jnp.logical_and(up_x, up_y))

    halo_in = (
        (disp.at[:, 0], disp_x), (disp_row, disp_y), (disp_edge, disp_c),
        (vel.at[:, 0], vel_x), (vel_row, vel_y), (vel_edge, vel_c),
    )
    halo_out = ((force_x, from_x), (force_y, from_y), (force_c, from_c))

    def start(copies, sends, recvs, to, allowed, which):
        for n in which:
            src, dst = copies[n]

            @pl.when(allowed[n % 3])
            def _():
                remote(src, dst, sends.at[n], recvs.at[n], to[n % 3]).start()

    def finish(copies, sends, recvs, to, sent, got, which):
        for n in which:
            src, dst = copies[n]

            @pl.when(got[n % 3])
            def _():
                remote(src, dst, sends.at[n], recvs.at[n], to[n % 3]).wait_recv()

            @pl.when(sent[n % 3])
            def _():
                remote(src, dst, sends.at[n], recvs.at[n], to[n % 3]).wait_send()

            @pl.when(jnp.logical_not(got[n % 3]))
            def _():
                dst[...] = jnp.zeros(dst.shape, F32)

    def scatter(outgoing, incoming, n):
        used = pl.ds(0, kept[n])

        @pl.loop(1, devices)
        def _(step):
            other, to = peer(step)
            remote(
                outgoing.at[other, used], incoming.at[me, used], slot_send.at[n], slot_recv.at[n], to
            ).start()

        incoming[me] = outgoing[me]

    def gather(outgoing, incoming, n):
        most = (pl.ds(0, devices - 1), pl.ds(0, kept[n]))
        whole = remote(
            outgoing.at[most], incoming.at[most], slot_send.at[n], slot_recv.at[n], peer(1)[1]
        )
        whole.wait_send()
        whole.wait_recv()

    halo = (halo_in, halo_send, halo_recv, below)
    start(*halo, has_below, (0, 1, 2))
    loads[1].wait()
    loads[2].wait()
    index_kernel(devices, capacity, size_x, size_y, size_z, elem, bucket, index)
    inner_faces(chunk, disp, index, faces, payload, hot_depth, hot_low)
    finish(*halo, has_below, has_above, (0, 1, 2))
    to_messages(
        all_faces(
            chunk, disp, disp_last, disp_x, disp_y, disp_c, index, groups, edges, payload,
            hot_depth, hot_low,
        ),
        slots_out,
    )
    scatter(slots_out, slots_in, 0)
    loads[3].wait()
    pack(vel, vel_row, vel_edge)
    start(*halo, has_below, (3, 4, 5))
    for load in loads[4:]:
        load.wait()
    for k in range(candidates.shape[0]):
        hot_slot[k] = bf16_hot(split_index(candidates[k : k + 1], LANES)[1], LANES)
    finish(*halo, has_below, has_above, (3, 4, 5))
    stress_kernel(
        vel, vel_x, vel_y, vel_c, stress, lame_lambda, lame_mu,
        new_stress, force, force_x, force_y, force_c,
    )
    store = pltpu.make_async_copy(new_stress, stress_out, store_sem)
    store.start()
    gather(slots_out, slots_in, 0)
    to_messages(contact(from_messages(slots_in), points, candidates, hot_slot, slave_force), back_out)
    scatter(back_out, back_in, 1)
    gather(back_out, back_in, 1)
    nodes_kernel(
        chunk, from_messages(back_in), index, hot_depth, hot_low, force, force_x, force_y, force_c
    )
    back = (halo_out, force_send, force_recv, above)
    start(*back, has_above, (0, 1, 2))
    finish(*back, has_above, has_below, (0, 1, 2))
    store.wait()


def per_device(
    velocity, stress, lame_lambda, lame_mu, node_mass, displacement,
    seg_elem, seg_bucket, slave_points, candidates,
):
    count_x = lax.axis_size("gx")
    count_y = lax.axis_size("gy")
    devices = count_x * count_y
    _, size_x, size_y, size_z = velocity.shape
    seg_count = seg_elem.shape[0]
    capacity = 2 * seg_count // devices
    chunk = min(512, seg_count)
    args = (
        displacement, seg_elem.reshape(1, seg_count), seg_bucket.reshape(1, seg_count),
        velocity, stress, lame_lambda, lame_mu, slave_points, candidates,
    )
    side_x, side_y, side_c = (3, size_y, size_z), (3, size_x, size_z), (3, size_z)
    outs = (stress.shape, velocity.shape, slave_points.shape, side_x, side_y, side_c)
    message = (devices, 8, capacity)
    scratch = [pltpu.VMEM(stress.shape, F32)] + [pltpu.VMEM(a.shape, a.dtype) for a in args]
    scratch += [
        pltpu.VMEM((8, seg_count), jnp.int32),
        pltpu.VMEM((size_z, seg_count), BF16),
        pltpu.VMEM((LANES, seg_count), BF16),
        pltpu.VMEM((candidates.shape[0], LANES, candidates.shape[1]), BF16),
    ]
    shapes = (
        [(6, size_x - 1, size_y, size_z), (6 * (size_x + size_y), size_z), (8, seg_count), side_y]
        + [side_x, side_y, side_c] * 2
        + [side_y, side_c] * 2
        + [message] * 4
        + [side_x, side_y, side_c]
    )
    scratch += [pltpu.VMEM(s, F32) for s in shapes]
    scratch += [pltpu.SemaphoreType.DMA((len(args),)), pltpu.SemaphoreType.DMA]
    scratch += [pltpu.SemaphoreType.DMA((n,)) for n in (6, 6, 3, 3, 2, 2)]
    parts = pl.pallas_call(
        functools.partial(fused_kernel, count_x, count_y, chunk),
        out_shape=[jax.ShapeDtypeStruct(s, F32) for s in outs],
        in_specs=[HBM] * len(args),
        out_specs=[HBM] + [VMEM] * (len(outs) - 1),
        scratch_shapes=scratch,
        compiler_params=pltpu.CompilerParams(
            collective_id=0, has_side_effects=True, vmem_limit_bytes=60 * 1024 * 1024
        ),
    )(*args)
    stress_part, force, pushed, *from_others = parts
    new_stress, acceleration, slave_force = pl.pallas_call(
        final_kernel,
        out_shape=[jax.ShapeDtypeStruct(s, F32) for s in outs[:3]],
        in_specs=[HBM] * 7,
        out_specs=[HBM] * 3,
        scratch_shapes=[
            pltpu.VMEM(s, F32)
            for s in (velocity.shape, side_x, side_y, side_c, node_mass.shape, velocity.shape)
        ]
        + [pltpu.SemaphoreType.DMA((8,))],
        compiler_params=pltpu.CompilerParams(vmem_limit_bytes=60 * 1024 * 1024),
    )(stress_part, pushed, force, *from_others, node_mass)
    return (new_stress, acceleration, slave_force)


def solution(mesh):
    grid = P(None, "gx", "gy", None)
    cells = P("gx", "gy", None)
    return jax.shard_map(
        per_device,
        mesh=mesh,
        in_specs=(
            grid, grid, cells, cells, cells, grid,
            P(("gx", "gy")), P(("gx", "gy"), None), P(None, ("gx", "gy")), P(None, ("gx", "gy")),
        ),
        out_specs=(grid, grid, P(None, ("gx", "gy"))),
        check_vma=False,
    )
```

```python
import functools

import jax
import jax.numpy as jnp
from jax import lax
from jax.experimental import pallas as pl
from jax.experimental.pallas import tpu as pltpu
from jax.sharding import PartitionSpec as P

time_step = 0.1
penalty = 10.0
LANES = 128
F32 = jnp.float32
BF16 = jnp.bfloat16
VMEM = pl.BlockSpec(memory_space=pltpu.VMEM)
HBM = pl.BlockSpec(memory_space=pltpu.HBM)
NN = (((1,), (0,)), ((), ()))
NT = (((1,), (1,)), ((), ()))


def split_index(value, size):
    if size & (size - 1) == 0:
        return value >> (size.bit_length() - 1), value & (size - 1)
    return value // size, value % size


def two_terms(value):
    high = value.astype(BF16)
    return high, (value - high.astype(F32)).astype(BF16)


def dot(left, right, dims):
    return lax.dot_general(left, right, dims, preferred_element_type=F32)


def stacked(terms, right, dims):
    rows = terms.shape[0] // 2
    both = dot(terms, right, dims)
    return both[:rows] + both[rows:]


def halves(total):
    rows = total.shape[0] // 2
    return total[:rows] + total[rows:]


def one_hot(row, count):
    return lax.broadcasted_iota(jnp.int32, (count, row.shape[1]), 0) == row


def next_row(tile, last):
    rows = tile.shape[0]
    rolled = pltpu.roll(tile, rows - 1, 0)
    return jnp.where(lax.broadcasted_iota(jnp.int32, tile.shape, 0) == rows - 1, last, rolled)


def previous_row(tile):
    rolled = pltpu.roll(tile, 1, 0)
    return jnp.where(lax.broadcasted_iota(jnp.int32, tile.shape, 0) == 0, 0.0, rolled)


def next_lane(tile):
    lanes = tile.shape[1]
    rolled = pltpu.roll(tile, lanes - 1, 1)
    return jnp.where(lax.broadcasted_iota(jnp.int32, tile.shape, 1) == lanes - 1, 0.0, rolled)


def previous_lane(tile):
    rolled = pltpu.roll(tile, 1, 1)
    return jnp.where(lax.broadcasted_iota(jnp.int32, tile.shape, 1) == 0, 0.0, rolled)


def index_kernel(devices, capacity, size_x, size_y, size_z, elem, bucket, out):
    count = elem.shape[1]
    row, depth = split_index(elem[...], size_z)
    cell_i, cell_j = split_index(row, size_y)
    ends = cell_j == size_y - 1
    out[0:1] = depth + 1
    out[1:2] = row
    out[4:5] = jnp.where(ends, -1, row)
    out[5:6] = row - (size_x - 1) * size_y
    out[6:7] = jnp.where(ends & (cell_i < size_x - 1), cell_i, -1)
    out[7:8] = jnp.zeros((1, count), jnp.int32)
    tri = (
        lax.broadcasted_iota(jnp.int32, (LANES, LANES), 0)
        <= lax.broadcasted_iota(jnp.int32, (LANES, LANES), 1)
    ).astype(F32).astype(BF16)
    carry = jnp.zeros((devices, 1), F32)
    for start in range(0, count, LANES):
        here = bucket[:, start : start + LANES]
        hot = one_hot(here, devices).astype(F32)
        running = dot(hot.astype(BF16), tri, NN)
        rank = jnp.sum(hot * (running + carry), axis=0, keepdims=True) - 1.0
        carry = carry + running[:, LANES - 1 : LANES]
        target = here * capacity + rank.astype(jnp.int32)
        high, low = split_index(target, LANES)
        out[2:3, start : start + LANES] = high
        out[3:4, start : start + LANES] = low


def spread(values, high, groups):
    rows, lanes = values.shape
    which = lax.broadcasted_iota(jnp.int32, (groups, rows, lanes), 0)
    kept = jnp.where(which == high[None], values[None], 0.0)
    return kept.reshape(groups * rows, lanes)


def spread_terms(values, high, groups):
    part = values.astype(BF16).astype(F32)
    return jnp.concatenate(
        [spread(term, high, groups).astype(BF16) for term in (part, values - part)], 0
    )


def picked(table, high, groups):
    rows = table.shape[0] // groups
    lanes = table.shape[1]
    total = jnp.zeros((rows, lanes), F32)
    for group in range(groups):
        total = jnp.where(high == group, table[group * rows : (group + 1) * rows], total)
    return total


def face_values(low, high, low_next, high_next):
    mean = [0.25 * ((low[c] + high[c]) + (low_next[c] + high_next[c])) for c in range(3)]
    p = [high_next[c] - low[c] for c in range(3)]
    q = [low_next[c] - high[c] for c in range(3)]
    return mean + [
        0.5 * ((1.0 + p[1]) * q[2] - p[2] * (1.0 + q[1])),
        0.5 * (p[2] * (q[0] - 1.0) - (1.0 + p[0]) * q[2]),
        0.5 * (p[0] + p[1] + q[1] - q[0] + p[0] * q[1] - p[1] * q[0]),
    ]


def chosen(table, hot_row, at):
    rows = hot_row.shape[0]
    return jnp.sum(jnp.where(hot_row, table[at : at + rows], 0.0), axis=0, keepdims=True)


def bf16_hot(row, count):
    return one_hot(row, count).astype(F32).astype(BF16)


def inner_faces(chunk, own, index, faces, payload, hot_depth, hot_low):
    size_x, size_y, size_z = own.shape[1:]
    count = index.shape[1]
    for i in range(size_x - 1):
        low = [own[c, i] for c in range(3)]
        high = [own[c, i + 1] for c in range(3)]
        after = [pltpu.roll(t, size_y - 1, 0) for t in low]
        high_after = [pltpu.roll(t, size_y - 1, 0) for t in high]
        for number, value in enumerate(face_values(low, high, after, high_after)):
            faces[number, i] = value
    rows = (size_x - 1) * size_y
    high, low = two_terms(faces[...].reshape(6 * rows, size_z))
    for start in range(0, count, chunk):
        here = slice(start, start + chunk)
        hot = bf16_hot(index[0:1, here], size_z)
        hot_depth[:, here] = hot
        hot_low[:, here] = bf16_hot(index[3:4, here], LANES)
        near = dot(high, hot, NN) + dot(low, hot, NN)
        hot_row = one_hot(index[4:5, here], rows)
        for comp in range(6):
            payload[comp : comp + 1, here] = chosen(near, hot_row, comp * rows)
    payload[6:7] = jnp.ones((1, count), F32)
    payload[7:8] = jnp.zeros((1, count), F32)


def all_faces(
    chunk, own, own_last, ghost_x, ghost_y, ghost_c, index, groups, edges, payload, hot_depth, hot_low
):
    size_x, size_y, size_z = own.shape[1:]
    count = index.shape[1]
    low = [own[c, size_x - 1] for c in range(3)]
    high = [ghost_x[c] for c in range(3)]
    after = [next_row(low[c], ghost_y[c, size_x - 1 : size_x]) for c in range(3)]
    high_after = [next_row(high[c], ghost_c[c : c + 1]) for c in range(3)]
    at = 0
    for value in face_values(low, high, after, high_after):
        edges[at : at + size_y] = value
        at += size_y
    low = [own_last[c] for c in range(3)]
    after = [ghost_y[c] for c in range(3)]
    high = [pltpu.roll(t, size_x - 1, 0) for t in low]
    high_after = [pltpu.roll(t, size_x - 1, 0) for t in after]
    for value in face_values(low, high, after, high_after):
        edges[at : at + size_x] = value
        at += size_x
    terms = jnp.concatenate(two_terms(edges[...]), 0)
    total = jnp.zeros((groups * 16, LANES), F32)
    for start in range(0, count, chunk):
        here = slice(start, start + chunk)
        near = stacked(terms, hot_depth[:, here], NN)
        hot_x = one_hot(index[5:6, here], size_y)
        hot_y = one_hot(index[6:7, here], size_x)
        for comp in range(6):
            payload[comp : comp + 1, here] += chosen(near, hot_x, comp * size_y) + chosen(
                near, hot_y, 6 * size_y + comp * size_x
            )
        slot = index[2:3, here]
        values = payload[:, here]
        total += dot(spread_terms(values, slot, groups), hot_low[:, here], NT)
    return halves(total)


def stress_kernel(
    own, ghost_x, ghost_y, ghost_c, stress, lame_lambda, lame_mu,
    new_stress, force, force_x, force_y, force_c,
):
    size_x = own.shape[1]
    size_y = own.shape[2]

    def plane(comp, i):
        tile = own[comp, i] if i < size_x else ghost_x[comp]
        last = ghost_y[comp, i : i + 1] if i < size_x else ghost_c[comp : comp + 1]
        after = next_row(tile, last)
        both, change = tile + after, after - tile
        return both + next_lane(both), change + next_lane(change), next_lane(both) - both

    low = [plane(comp, 0) for comp in range(3)]
    carry = None
    for i in range(size_x):
        high = [plane(comp, i + 1) for comp in range(3)]
        grad_x = [high[c][0] - low[c][0] for c in range(3)]
        grad_y = [high[c][1] + low[c][1] for c in range(3)]
        grad_z = [high[c][2] + low[c][2] for c in range(3)]
        low = high
        shear = (0.5 * time_step) * lame_mu[i]
        volume = (0.25 * time_step) * lame_lambda[i] * (grad_x[0] + grad_y[1] + grad_z[2])
        s_xx = stress[0, i] + (volume + shear * grad_x[0])
        s_yy = stress[1, i] + (volume + shear * grad_y[1])
        s_zz = stress[2, i] + (volume + shear * grad_z[2])
        half = 0.5 * shear
        s_yz = stress[3, i] + half * (grad_z[1] + grad_y[2])
        s_xz = stress[4, i] + half * (grad_z[0] + grad_x[2])
        s_xy = stress[5, i] + half * (grad_y[0] + grad_x[1])
        for number, value in enumerate((s_xx, s_yy, s_zz, s_yz, s_xz, s_xy)):
            new_stress[number, i] = value
        tensor = ((s_xx, s_xy, s_xz), (s_xy, s_yy, s_yz), (s_xz, s_yz, s_zz))
        later = []
        for comp in range(3):
            first, second, third = (-0.25 * t for t in tensor[comp])
            first = first + previous_lane(first)
            second = second + previous_lane(second)
            third = previous_lane(third) - third
            near_plus, near_minus = third - second + first, third - second - first
            far_plus, far_minus = third + second + first, third + second - first
            plus = near_plus + previous_row(far_plus)
            minus = near_minus + previous_row(far_minus)
            plus_end = far_plus[size_y - 1 : size_y]
            minus_end = far_minus[size_y - 1 : size_y]
            if carry is not None:
                minus = minus + carry[comp][0]
                minus_end = minus_end + carry[comp][1]
            force[comp, i] = minus
            force_y[comp, i : i + 1] = minus_end
            later.append((plus, plus_end))
        carry = later
    for comp in range(3):
        force_x[comp] = carry[comp][0]
        force_c[comp : comp + 1] = carry[comp][1]


def contact(arrived, points, candidates, hot_slot, slave_force):
    groups = arrived.shape[0] // 8
    lanes = points.shape[1]
    terms = jnp.concatenate(two_terms(arrived), 0)
    total = jnp.zeros((groups * 16, LANES), F32)
    pushed = [jnp.zeros((1, lanes), F32) for _ in range(3)]
    eight = lax.broadcasted_iota(jnp.int32, (8, lanes), 0)
    for k in range(candidates.shape[0]):
        slot = split_index(candidates[k : k + 1], LANES)[0]
        hot = hot_slot[k]
        near = picked(stacked(terms, hot, NN), slot, groups)
        rows = [near[r : r + 1] for r in range(7)]
        filled = rows[6]
        offset = (0.5, 0.5, 1.0)
        area = (rows[3], rows[4], rows[5] + filled)
        gap = jnp.zeros((1, lanes), F32)
        for comp in range(3):
            gap = gap + area[comp] * (points[comp : comp + 1] - (rows[comp] + offset[comp] * filled))
        scale = penalty * jnp.maximum(-gap, 0.0)
        values = jnp.zeros((8, lanes), F32)
        for comp in range(3):
            push = scale * area[comp]
            pushed[comp] = pushed[comp] + push
            values = jnp.where(eight == comp, -push, values)
        total += dot(spread_terms(values, slot, groups), hot, NT)
    for comp in range(3):
        slave_force[comp : comp + 1] = pushed[comp]
    return halves(total)


def nodes_kernel(
    chunk, returned, index, hot_depth, hot_low, force, force_x, force_y, force_c
):
    size_x, size_y, size_z = force.shape[1:]
    groups = returned.shape[0] // 8
    count = index.shape[1]
    rows = size_x * size_y
    terms = jnp.concatenate(two_terms(returned), 0)
    total = jnp.zeros((6 * rows, size_z), F32)
    for start in range(0, count, chunk):
        here = slice(start, start + chunk)
        near = picked(stacked(terms, hot_low[:, here], NN), index[2:3, here], groups)
        quarter = 0.25 * near
        part = quarter.astype(BF16).astype(F32)
        rest = quarter - part
        hot_row = one_hot(index[1:2, here], rows)
        left = jnp.concatenate(
            [
                jnp.where(hot_row, values[c : c + 1], 0.0)
                for values in (part, rest)
                for c in range(3)
            ],
            0,
        ).astype(BF16)
        total += dot(left, hot_depth[:, here], NT)
    total = halves(total)
    for comp in range(3):
        before = None
        for i in range(size_x):
            at = (comp * size_x + i) * size_y
            tile = total[at : at + size_y]
            both = tile + previous_row(tile)
            end = tile[size_y - 1 : size_y]
            value, value_end = both, end
            if before is not None:
                value, value_end = both + before[0], end + before[1]
            force[comp, i] = force[comp, i] + value
            force_y[comp, i : i + 1] = force_y[comp, i : i + 1] + value_end
            before = (both, end)
        force_x[comp] = force_x[comp] + before[0]
        force_c[comp : comp + 1] = force_c[comp : comp + 1] + before[1]


def final_kernel(
    stress, pushed, force_in, from_x_in, from_y_in, from_c_in, mass_in,
    new_stress, acceleration, slave_force,
    stress_here, pushed_here, force, from_x, from_y, from_c, mass, result, sems,
):
    copies = [
        pltpu.make_async_copy(src, dst, sems.at[n])
        for n, (src, dst) in enumerate(
            (
                (stress, stress_here), (pushed, pushed_here), (mass_in, mass), (force_in, force),
                (from_x_in, from_x), (from_y_in, from_y), (from_c_in, from_c),
                (stress_here, new_stress), (pushed_here, slave_force), (result, acceleration),
            )
        )
    ]
    for copy in copies[:7]:
        copy.start()
    for n in (0, 1):
        copies[n].wait()
        copies[7 + n].start()
    for copy in copies[2:7]:
        copy.wait()
    size_x = force.shape[1]
    first = lax.broadcasted_iota(jnp.int32, force.shape[2:], 0) == 0
    for i in range(size_x):
        inverse = 1.0 / mass[i]
        for comp in range(3):
            end = from_y[comp, i : i + 1]
            value = force[comp, i]
            if i == 0:
                end = end + from_c[comp : comp + 1]
                value = value + from_x[comp]
            result[comp, i] = (value + jnp.where(first, end, 0.0)) * inverse
    copies[9].start()
    for copy in copies[7:]:
        copy.wait()


def to_messages(total, messages):
    devices, rows, capacity = messages.shape
    per = LANES // capacity
    if per == 1:
        messages[...] = total.reshape(messages.shape)
        return
    for device in range(devices):
        group, part = device // per, device % per
        messages[device] = total[
            group * rows : (group + 1) * rows, part * capacity : (part + 1) * capacity
        ]


def from_messages(messages):
    devices, rows, capacity = messages.shape
    per = LANES // capacity
    if per == 1:
        return messages[...].reshape(devices * rows, LANES)
    return jnp.concatenate(
        [
            jnp.concatenate([messages[group * per + part] for part in range(per)], 1)
            for group in range(devices // per)
        ],
        0,
    )


def fused_kernel(
    count_x, count_y, chunk,
    disp_in, elem_in, bucket_in, vel_in, stress_in, lambda_in, mu_in, points_in, candidates_in,
    stress_out, force, slave_force, from_x, from_y, from_c,
    new_stress, disp, elem, bucket, vel, stress, lame_lambda, lame_mu, points, candidates,
    index, hot_depth, hot_low, hot_slot, faces, edges, payload, disp_last,
    disp_x, disp_y, disp_c, vel_x, vel_y, vel_c,
    disp_row, disp_edge, vel_row, vel_edge,
    slots_out, slots_in, back_out, back_in,
    force_x, force_y, force_c,
    load_sems, store_sem, halo_send, halo_recv, force_send, force_recv, slot_send, slot_recv,
):
    devices = count_x * count_y
    _, size_x, size_y, size_z = vel.shape
    capacity = slots_out.shape[2]
    groups = devices * capacity // LANES
    kept = (7, 3)
    at_x, at_y = lax.axis_index("gx"), lax.axis_index("gy")
    me = at_x * count_y + at_y

    def peer(step):
        other = lax.rem(me + step, devices)
        return other, (lax.div(other, count_y), lax.rem(other, count_y))

    def remote(src, dst, send, recv, to):
        return pltpu.make_async_remote_copy(
            src_ref=src, dst_ref=dst, send_sem=send, recv_sem=recv,
            device_id=to, device_id_type=pl.DeviceIdType.MESH,
        )

    loads = [
        pltpu.make_async_copy(src, dst, load_sems.at[n])
        for n, (src, dst) in enumerate(
            (
                (disp_in, disp), (elem_in, elem), (bucket_in, bucket), (vel_in, vel),
                (stress_in, stress), (lambda_in, lame_lambda), (mu_in, lame_mu),
                (points_in, points), (candidates_in, candidates),
            )
        )
    ]
    for load in loads:
        load.start()
    barrier = pltpu.get_barrier_semaphore()

    @pl.loop(1, devices)
    def _(step):
        pl.semaphore_signal(
            barrier, inc=1, device_id=peer(step)[1], device_id_type=pl.DeviceIdType.MESH
        )

    def pack(own, row, edge):
        for comp in range(3):
            for i in range(size_x):
                row[comp, i : i + 1] = own[comp, i, 0:1]
            edge[comp : comp + 1] = own[comp, 0, 0:1]

    loads[0].wait()
    pack(disp, disp_row, disp_edge)
    for comp in range(3):
        for i in range(size_x):
            disp_last[comp, i : i + 1] = disp[comp, i, size_y - 1 : size_y]
    pl.semaphore_wait(barrier, devices - 1)

    down_x, down_y = at_x > 0, at_y > 0
    up_x, up_y = at_x < count_x - 1, at_y < count_y - 1
    below = ((at_x - 1, at_y), (at_x, at_y - 1), (at_x - 1, at_y - 1))
    above = ((at_x + 1, at_y), (at_x, at_y + 1), (at_x + 1, at_y + 1))
    has_below = (down_x, down_y, jnp.logical_and(down_x, down_y))
    has_above = (up_x, up_y, jnp.logical_and(up_x, up_y))

    halo_in = (
        (disp.at[:, 0], disp_x), (disp_row, disp_y), (disp_edge, disp_c),
        (vel.at[:, 0], vel_x), (vel_row, vel_y), (vel_edge, vel_c),
    )
    halo_out = ((force_x, from_x), (force_y, from_y), (force_c, from_c))

    def start(copies, sends, recvs, to, allowed, which):
        for n in which:
            src, dst = copies[n]

            @pl.when(allowed[n % 3])
            def _():
                remote(src, dst, sends.at[n], recvs.at[n], to[n % 3]).start()

    def finish(copies, sends, recvs, to, sent, got, which):
        for n in which:
            src, dst = copies[n]

            @pl.when(got[n % 3])
            def _():
                remote(src, dst, sends.at[n], recvs.at[n], to[n % 3]).wait_recv()

            @pl.when(sent[n % 3])
            def _():
                remote(src, dst, sends.at[n], recvs.at[n], to[n % 3]).wait_send()

            @pl.when(jnp.logical_not(got[n % 3]))
            def _():
                dst[...] = jnp.zeros(dst.shape, F32)

    def scatter(outgoing, incoming, n):
        used = pl.ds(0, kept[n])

        @pl.loop(1, devices)
        def _(step):
            other, to = peer(step)
            remote(
                outgoing.at[other, used], incoming.at[me, used], slot_send.at[n], slot_recv.at[n], to
            ).start()

        incoming[me] = outgoing[me]

    def gather(outgoing, incoming, n):
        most = (pl.ds(0, devices - 1), pl.ds(0, kept[n]))
        whole = remote(
            outgoing.at[most], incoming.at[most], slot_send.at[n], slot_recv.at[n], peer(1)[1]
        )
        whole.wait_send()
        whole.wait_recv()

    halo = (halo_in, halo_send, halo_recv, below)
    start(*halo, has_below, (0, 1, 2))
    loads[1].wait()
    loads[2].wait()
    index_kernel(devices, capacity, size_x, size_y, size_z, elem, bucket, index)
    inner_faces(chunk, disp, index, faces, payload, hot_depth, hot_low)
    finish(*halo, has_below, has_above, (0, 1, 2))
    to_messages(
        all_faces(
            chunk, disp, disp_last, disp_x, disp_y, disp_c, index, groups, edges, payload,
            hot_depth, hot_low,
        ),
        slots_out,
    )
    scatter(slots_out, slots_in, 0)
    loads[3].wait()
    pack(vel, vel_row, vel_edge)
    start(*halo, has_below, (3, 4, 5))
    for load in loads[4:]:
        load.wait()
    for k in range(candidates.shape[0]):
        hot_slot[k] = bf16_hot(split_index(candidates[k : k + 1], LANES)[1], LANES)
    finish(*halo, has_below, has_above, (3, 4, 5))
    stress_kernel(
        vel, vel_x, vel_y, vel_c, stress, lame_lambda, lame_mu,
        new_stress, force, force_x, force_y, force_c,
    )
    store = pltpu.make_async_copy(new_stress, stress_out, store_sem)
    store.start()
    gather(slots_out, slots_in, 0)
    to_messages(contact(from_messages(slots_in), points, candidates, hot_slot, slave_force), back_out)
    scatter(back_out, back_in, 1)
    gather(back_out, back_in, 1)
    nodes_kernel(
        chunk, from_messages(back_in), index, hot_depth, hot_low, force, force_x, force_y, force_c
    )
    back = (halo_out, force_send, force_recv, above)
    start(*back, has_above, (0, 1, 2))
    finish(*back, has_above, has_below, (0, 1, 2))
    store.wait()


def per_device(
    velocity, stress, lame_lambda, lame_mu, node_mass, displacement,
    seg_elem, seg_bucket, slave_points, candidates,
):
    count_x = lax.axis_size("gx")
    count_y = lax.axis_size("gy")
    devices = count_x * count_y
    _, size_x, size_y, size_z = velocity.shape
    seg_count = seg_elem.shape[0]
    capacity = 2 * seg_count // devices
    chunk = min(512, seg_count)
    args = (
        displacement, seg_elem.reshape(1, seg_count), seg_bucket.reshape(1, seg_count),
        velocity, stress, lame_lambda, lame_mu, slave_points, candidates,
    )
    side_x, side_y, side_c = (3, size_y, size_z), (3, size_x, size_z), (3, size_z)
    outs = (stress.shape, velocity.shape, slave_points.shape, side_x, side_y, side_c)
    message = (devices, 8, capacity)
    scratch = [pltpu.VMEM(stress.shape, F32)] + [pltpu.VMEM(a.shape, a.dtype) for a in args]
    scratch += [
        pltpu.VMEM((8, seg_count), jnp.int32),
        pltpu.VMEM((size_z, seg_count), BF16),
        pltpu.VMEM((LANES, seg_count), BF16),
        pltpu.VMEM((candidates.shape[0], LANES, candidates.shape[1]), BF16),
    ]
    shapes = (
        [(6, size_x - 1, size_y, size_z), (6 * (size_x + size_y), size_z), (8, seg_count), side_y]
        + [side_x, side_y, side_c] * 2
        + [side_y, side_c] * 2
        + [message] * 4
        + [side_x, side_y, side_c]
    )
    scratch += [pltpu.VMEM(s, F32) for s in shapes]
    scratch += [pltpu.SemaphoreType.DMA((len(args),)), pltpu.SemaphoreType.DMA]
    scratch += [pltpu.SemaphoreType.DMA((n,)) for n in (6, 6, 3, 3, 2, 2)]
    parts = pl.pallas_call(
        functools.partial(fused_kernel, count_x, count_y, chunk),
        out_shape=[jax.ShapeDtypeStruct(s, F32) for s in outs],
        in_specs=[HBM] * len(args),
        out_specs=[HBM] + [VMEM] * (len(outs) - 1),
        scratch_shapes=scratch,
        compiler_params=pltpu.CompilerParams(
            collective_id=0, has_side_effects=True, vmem_limit_bytes=60 * 1024 * 1024
        ),
    )(*args)
    stress_part, force, pushed, *from_others = parts
    new_stress, acceleration, slave_force = pl.pallas_call(
        final_kernel,
        out_shape=[jax.ShapeDtypeStruct(s, F32) for s in outs[:3]],
        in_specs=[HBM] * 7,
        out_specs=[HBM] * 3,
        scratch_shapes=[
            pltpu.VMEM(s, F32)
            for s in outs[:1] + outs[2:3] + (velocity.shape, side_x, side_y, side_c, node_mass.shape, velocity.shape)
        ]
        + [pltpu.SemaphoreType.DMA((10,))],
        compiler_params=pltpu.CompilerParams(vmem_limit_bytes=60 * 1024 * 1024),
    )(stress_part, pushed, force, *from_others, node_mass)
    return (new_stress, acceleration, slave_force)


def solution(mesh):
    grid = P(None, "gx", "gy", None)
    cells = P("gx", "gy", None)
    return jax.shard_map(
        per_device,
        mesh=mesh,
        in_specs=(
            grid, grid, cells, cells, cells, grid,
            P(("gx", "gy")), P(("gx", "gy"), None), P(None, ("gx", "gy")), P(None, ("gx", "gy")),
        ),
        out_specs=(grid, grid, P(None, ("gx", "gy"))),
        check_vma=False,
    )
```
